256 devices in a mesh: tm: 8 (over y, core), space: 32 (over z, x).
Axes of the slice: x: 4, y: 4, z: 8, core: 2. Of those that a mesh axis runs over, the one named last changes fastest.
Arguments:
- feats: bfloat16 [32, 64, 80, 384], P('tm', 'space'), may hold values from -6 to 6
- clip_lengths: int32 [3], replicated, may hold values from 1 to 16, as said below
- norm_gain: float32 [384], replicated, may hold values from 0.1 to 1.9
- conv_weight: bfloat16 [3, 3, 3, 384, 384], replicated, may hold values from -0.109375 to 0.109375
- conv_bias: float32 [384], replicated, may hold values from -3 to 3
- attn_gain: float32 [384], replicated, may hold values from 0.1 to 1.9
- query_weight: bfloat16 [384, 384], replicated, may hold values from -4 to 4
- key_weight: bfloat16 [384, 384], replicated, may hold values from -4 to 4
- value_weight: bfloat16 [384, 384], replicated, may hold values from -0.3125 to 0.3125
- output_weight: bfloat16 [384, 384], replicated, may hold values from -0.3125 to 0.3125
Outputs:
- resid: bfloat16 [32, 64, 80, 384], P('tm', 'space')
- mixed: bfloat16 [32, 64, 80, 384], P('tm', 'space')
The draws below stay inside these ranges and needn't reach their ends.
Inputs may be any that keep to these rules, and one draw needn't show every extreme that they name: `clip_lengths`: the lengths sum to 32; exactly one clip has 16 frames.
All inputs are finite; a program needn't handle non-finite values.
Results may differ from the reference program's by a relative error of at most 0.0085.
Values may be sent and summed in bfloat16 or wider, within the bound.
A program may use at most 128 MiB of HBM per device.

```python
import math
import jax
import jax.numpy as jnp
from jax import lax

C = 384
WID = 80
FRAMES = 32
HGT = 64
N_SPACE = 32


def draw_clip_lengths(key, part):
    key = jax.random.fold_in(key, 5)
    split_key, order_key = jax.random.split(key)
    half_frames = FRAMES // 2
    split_point = jax.random.randint(split_key, (), 1, half_frames, dtype=jnp.int32)
    pieces = jnp.stack([jnp.int32(half_frames), split_point, FRAMES - half_frames - split_point]).astype(jnp.int32)
    order = jax.random.permutation(order_key, 3)
    return pieces[order].astype(jnp.int32)


def draw_query_weight(key, part):
    key = jax.random.fold_in(key, 7)
    own_matrix = jax.random.normal(key, (C, C), jnp.float32)
    matrix = own_matrix
    return jnp.clip(matrix * (3.0 / C) ** 0.5, -4.0, 4.0).astype(jnp.bfloat16)


def draw_key_weight(key, part):
    key = jax.random.fold_in(key, 9)
    own_matrix = jax.random.normal(key, (C, C), jnp.float32)
    matrix = own_matrix
    return jnp.clip(matrix * (3.0 / C) ** 0.5, -4.0, 4.0).astype(jnp.bfloat16)


def steps_of(key, shape, cuts, least, largest):
    level = 1.0
    for axis_at, blocks in cuts:
        steps = jax.random.uniform(jax.random.fold_in(jax.random.fold_in(key, 6), axis_at), (blocks,), jnp.float32, least / len(cuts), largest / len(cuts))
        level = level * jnp.repeat(jnp.exp(steps), shape[axis_at] // blocks).reshape((-1,) + (1,) * (len(shape) - 1 - axis_at))
    return level


def gaussian(key, extent, spread, limit, cuts=(), kind=jnp.bfloat16):
    level = steps_of(key, extent, cuts, -0.22, 0.18) if cuts else 1.0
    array = jax.random.normal(key, extent, jnp.float32) * spread * level
    return jnp.minimum(jnp.maximum(array, -limit), limit).astype(kind)


def setup_inputs(seed: int = 0) -> dict:
    key_of = jax.random.split(jax.random.key(seed), 11)
    return {
        "feats": gaussian(key_of[0], (FRAMES, HGT, WID, C), 1.0, 6.0, ((0, 8), (1, 32))),
        "clip_lengths": draw_clip_lengths(jax.random.fold_in(key_of[10], 71), 0),
        "norm_gain": jnp.clip(1.0 + 0.18 * jax.random.normal(key_of[2], (C,), jnp.float32), 0.1, 1.9),
        "conv_weight": gaussian(key_of[3], (3, 3, 3, C, C), (9 * C) ** -0.5, 0.109375),
        "conv_bias": gaussian(key_of[4], (C,), 0.5, 3.0, (), jnp.float32),
        "attn_gain": jnp.clip(1.0 + 0.18 * jax.random.normal(key_of[5], (C,), jnp.float32), 0.1, 1.9),
        "query_weight": draw_query_weight(jax.random.fold_in(key_of[10], 71), 0),
        "key_weight": draw_key_weight(jax.random.fold_in(key_of[10], 71), 0),
        "value_weight": gaussian(key_of[8], (C, C), C ** -0.5, 0.3125),
        "output_weight": gaussian(key_of[9], (C, C), C ** -0.5, 0.3125),
    }


def normalize(values, scale_gain):
    widened = values.astype(jnp.float32)
    return widened * lax.rsqrt(lax.optimization_barrier(jnp.mean(widened * widened, axis=-1, keepdims=True)) + 1e-06) * scale_gain

def frame_attention(frame_rows):
    query_rows, key_rows, value_rows = frame_rows
    block_count = N_SPACE // 4
    query_blocks = query_rows.reshape(block_count, -1, C)

    def one_block(query_block):
        scores = jnp.dot(query_block, key_rows.T, preferred_element_type=jnp.float32) / math.sqrt(C)
        top_score = lax.optimization_barrier(jnp.max(scores, axis=-1, keepdims=True))
        expanded = jnp.exp(scores - top_score)
        row_total = lax.optimization_barrier(jnp.sum(expanded, axis=-1, keepdims=True))
        weights = expanded.astype(jnp.bfloat16)
        summed = jnp.dot(weights, value_rows, preferred_element_type=jnp.float32)
        return (summed / row_total).astype(jnp.bfloat16)
    return lax.map(one_block, query_blocks).reshape(-1, C)

def reference(feats, clip_lengths, norm_gain, conv_weight, conv_bias, attn_gain, query_weight, key_weight, value_weight, output_weight):
    active = jax.nn.silu(normalize(feats, norm_gain)).astype(jnp.bfloat16)
    frame_ids = jnp.arange(FRAMES, dtype=jnp.int32)
    clip_ends = jnp.cumsum(clip_lengths).astype(jnp.int32)
    clip_starts = lax.optimization_barrier(jnp.sum(clip_lengths[None, :] * (clip_ends[None, :] <= frame_ids[:, None]).astype(jnp.int32), axis=1))
    padded = jnp.pad(active, ((2, 0), (1, 1), (1, 1), (0, 0)))
    conv_sum = jnp.zeros((FRAMES * HGT * WID, C), jnp.float32)
    for time_lag in range(3):
        live_mask = (frame_ids - time_lag >= clip_starts).astype(jnp.bfloat16)[:, None, None, None]
        for row_offset in range(3):
            for col_offset in range(3):
                window = padded[2 - time_lag:2 - time_lag + FRAMES, row_offset:row_offset + HGT, col_offset:col_offset + WID] * live_mask
                conv_sum = conv_sum + jnp.dot(window.reshape(-1, C), conv_weight[time_lag, row_offset, col_offset], preferred_element_type=jnp.float32)
    resid_flat = (feats.astype(jnp.float32).reshape(-1, C) + conv_sum + conv_bias).astype(jnp.bfloat16)
    normed = normalize(resid_flat, attn_gain).astype(jnp.bfloat16)
    queries = jnp.dot(normed, query_weight, preferred_element_type=jnp.float32).astype(jnp.bfloat16).reshape(FRAMES, HGT * WID, C)
    keys = jnp.dot(normed, key_weight, preferred_element_type=jnp.float32).astype(jnp.bfloat16).reshape(FRAMES, HGT * WID, C)
    values = jnp.dot(normed, value_weight, preferred_element_type=jnp.float32).astype(jnp.bfloat16).reshape(FRAMES, HGT * WID, C)
    attended = lax.map(frame_attention, (queries, keys, values)).reshape(-1, C)
    mixed = (resid_flat.astype(jnp.float32) + jnp.dot(attended, output_weight, preferred_element_type=jnp.float32)).astype(jnp.bfloat16)
    return (resid_flat.reshape(FRAMES, HGT, WID, C), mixed.reshape(FRAMES, HGT, WID, C))
```

```python
import math

import jax
import jax.numpy as jnp
from jax import lax
from jax.experimental import pallas as pl
from jax.experimental.pallas import tpu as pltpu
from jax.sharding import PartitionSpec as P

MESH = pl.DeviceIdType.MESH
COLS = 80
BLK = 2 * COLS
NB = 4
ROWS = NB * BLK
TILE = 320


def scaled(wide, gain):
    mean = jnp.mean(wide * wide, axis=-1, keepdims=True)
    return wide * lax.rsqrt(mean + 1e-06) * gain


def block_kernel(
    feats_ref, clip_ref, norm_gain_ref, conv_hbm, bias_ref, gain_ref, wq_ref, wk_ref, wv_ref, wo_ref,
    resid_ref, out_ref,
    weight, active, taps, conv, rin, kv, qs, acc, top, total, stage,
    w_sem, h_send, h_recv, a_send, a_recv, g_send, g_recv, r_send, r_recv,
):
    tm, space = lax.axis_index("tm"), lax.axis_index("space")
    y, c = tm // 2, tm % 2
    z, x = space // 4, space % 4
    right = (tm, 4 * z + (x + 1) % 4)
    left = (tm, 4 * z + (x + 3) % 4)
    sibling = (2 * y + 1 - c, space)
    slot, core = z % 4, z // 4
    above, below = (space + 31) % 32, (space + 1) % 32
    later, earlier = (tm + 1) % 8, (tm + 7) % 8
    channels = feats_ref.shape[-1]

    def partner(i):
        return (2 * y + core, 4 * (4 * c + i) + x)

    def remote(i):
        return 4 * c + i != z

    weight_copies = [
        pltpu.make_async_copy(conv_hbm.at[lag], weight.at[lag], w_sem.at[lag]) for lag in range(3)]
    for copy in weight_copies:
        copy.start()

    barrier = pltpu.get_barrier_semaphore()
    for device in (
        left, right, sibling, (tm, above), (tm, below), (later, space), (earlier, space),
        (later, above), (later, below), (earlier, above), (earlier, below),
    ):
        pl.semaphore_signal(barrier, inc=1, device_id=device, device_id_type=MESH)
    for i in range(NB):
        @pl.when(remote(i))
        def _(i=i):
            pl.semaphore_signal(barrier, inc=1, device_id=partner(i), device_id_type=MESH)

    norm_gain = norm_gain_ref[...]
    for frame in range(NB):
        for row in range(2):
            unit = scaled(feats_ref[frame, row].astype(jnp.float32), norm_gain)
            active[frame + 2, row + 1] = (unit / (1.0 + jnp.exp(-unit))).astype(jnp.bfloat16)

    @pl.when(core == c)
    def _():
        pl.semaphore_wait(barrier, 14)

    @pl.when(core != c)
    def _():
        pl.semaphore_wait(barrier, 15)

    own, recent = pl.ds(2, NB), pl.ds(NB, 2)
    first = pl.ds(0, 2)
    has_above, has_below, has_earlier, has_later = space > 0, space < 31, tm > 0, tm < 7

    def rim(k, source, target, device):
        return pltpu.make_async_remote_copy(
            src_ref=active.at[source[0], source[1]], dst_ref=active.at[target[0], target[1]],
            send_sem=h_send.at[k], recv_sem=h_recv.at[k], device_id=device, device_id_type=MESH)

    top_row, low_row, both_rows = pl.ds(1, 1), pl.ds(2, 1), pl.ds(1, 2)
    before_row, after_row = pl.ds(0, 1), pl.ds(3, 1)
    rims = [
        (has_below, has_above, rim(0, (own, low_row), (own, before_row), (tm, below)), (own, before_row)),
        (has_above, has_below, rim(1, (own, top_row), (own, after_row), (tm, above)), (own, after_row)),
        (has_later, has_earlier, rim(2, (recent, both_rows), (first, both_rows), (later, space)), (first, both_rows)),
        (jnp.logical_and(has_later, has_below), jnp.logical_and(has_earlier, has_above),
         rim(3, (recent, low_row), (first, before_row), (later, below)), (first, before_row)),
        (jnp.logical_and(has_later, has_above), jnp.logical_and(has_earlier, has_below),
         rim(4, (recent, top_row), (first, after_row), (later, above)), (first, after_row)),
    ]
    for sends_it, gets_it, copy, place in rims:
        @pl.when(sends_it)
        def _(copy=copy):
            copy.start()

        @pl.when(jnp.logical_not(gets_it))
        def _(place=place):
            hole = active.at[place[0], place[1]]
            hole[...] = jnp.zeros_like(hole)

    column = lax.broadcasted_iota(jnp.int32, (COLS, channels), 0)

    def spread(frame, row):
        middle = active[frame, row]
        wide = middle.astype(jnp.float32)
        taps[frame, row, :, 0:channels] = jnp.where(
            column == 0, 0.0, pltpu.roll(wide, 1, 0)).astype(jnp.bfloat16)
        taps[frame, row, :, channels:2 * channels] = middle
        taps[frame, row, :, 2 * channels:3 * channels] = jnp.where(
            column == COLS - 1, 0.0, pltpu.roll(wide, COLS - 1, 0)).astype(jnp.bfloat16)

    def product(lag, offset, start, stop):
        window = taps[start + 2 - lag:stop + 2 - lag, offset:offset + 2]
        return jnp.dot(
            window.reshape((stop - start) * BLK, 3 * channels), weight[lag, offset],
            preferred_element_type=jnp.float32)

    lengths = [clip_ref[k] for k in range(3)]
    ends = [lengths[0], lengths[0] + lengths[1], lengths[0] + lengths[1] + lengths[2]]

    def live(frame, lag):
        at = tm * NB + frame
        start = jnp.int32(0)
        for length, end in zip(lengths, ends):
            start = start + jnp.where(end <= at, length, 0)
        return at - lag >= start

    def add(lag, value, start, stop):
        for frame in range(start, stop):
            part = value[(frame - start) * BLK:(frame - start + 1) * BLK]
            if lag:
                part = jnp.where(live(frame, lag), part, 0.0)
            conv[frame] += part

    for frame in range(2, NB + 2):
        for row in (1, 2):
            spread(frame, row)
    for frame in range(NB):
        conv[frame] = (
            feats_ref[frame].reshape(BLK, channels).astype(jnp.float32) + bias_ref[...])
    for lag in range(3):
        weight_copies[lag].wait()
        add(lag, product(lag, 1, lag, NB), lag, NB)

    def received(k):
        gets_it, copy = rims[k][1], rims[k][2]

        @pl.when(gets_it)
        def _():
            copy.wait_recv()

    received(0)
    received(1)
    for frame in range(2, NB + 2):
        for row in (0, 3):
            spread(frame, row)
    for lag in range(3):
        add(lag, product(lag, 0, lag, NB) + product(lag, 2, lag, NB), lag, NB)

    def exchange(i, source, target, send_sem, recv_sem):
        return pltpu.make_async_remote_copy(
            src_ref=source.at[i], dst_ref=target.at[slot], send_sem=send_sem.at[i],
            recv_sem=recv_sem.at[slot], device_id=partner(i), device_id_type=MESH)

    def arrival(b, target, send_sem, recv_sem):
        return pltpu.make_async_remote_copy(
            src_ref=target.at[b], dst_ref=target.at[b], send_sem=send_sem.at[b],
            recv_sem=recv_sem.at[b], device_id=partner(b), device_id_type=MESH)

    def hand_over(i):
        resid_ref[i] = conv[i].astype(jnp.bfloat16)

        @pl.when(remote(i))
        def _():
            exchange(i, resid_ref, rin, a_send, a_recv).start()

        @pl.when(jnp.logical_not(remote(i)))
        def _():
            rin[i] = resid_ref[i]

    hand_over(2)
    hand_over(3)
    for k in (2, 3, 4):
        received(k)
    for frame in range(2):
        for row in range(4):
            spread(frame, row)
    add(2, product(2, 0, 0, 2) + product(2, 1, 0, 2) + product(2, 2, 0, 2), 0, 2)
    add(1, product(1, 0, 0, 1) + product(1, 1, 0, 1) + product(1, 2, 0, 1), 0, 1)
    hand_over(0)
    hand_over(1)

    sends = []

    def push(source, dest, device):
        (sc, sp), (dc, dp) = source, dest
        copy = pltpu.make_async_remote_copy(
            src_ref=kv.at[sc, pl.ds(sp * BLK, BLK)], dst_ref=kv.at[dc, pl.ds(dp * BLK, BLK)],
            send_sem=g_send.at[len(sends)], recv_sem=g_recv.at[dc * NB + dp],
            device_id=device, device_id_type=MESH)
        copy.start()
        sends.append(copy)

    def landed(chunk, place):
        pltpu.make_async_remote_copy(
            src_ref=kv.at[chunk, pl.ds(place * BLK, BLK)], dst_ref=kv.at[chunk, pl.ds(place * BLK, BLK)],
            send_sem=g_send.at[0], recv_sem=g_recv.at[chunk * NB + place],
            device_id=sibling, device_id_type=MESH).wait_recv()

    for b in range(NB):
        @pl.when(remote(b))
        def _(b=b):
            arrival(b, rin, a_send, a_recv).wait_recv()

        kv[0, b * BLK:(b + 1) * BLK] = scaled(rin[b].astype(jnp.float32), gain_ref[...]).astype(jnp.bfloat16)
        push((0, b), (2 + b, 0), right)
        push((0, b), (2 + b, 1), left)
        push((0, b), (1, b), sibling)

    queries = jnp.dot(kv[0], wq_ref[...], preferred_element_type=jnp.float32).astype(jnp.bfloat16)
    folded = lax.dot_general(
        queries, wk_ref[...], (((1,), (1,)), ((), ())), preferred_element_type=jnp.float32)
    qs[...] = (folded * (math.log2(math.e) / math.sqrt(folded.shape[-1]))).astype(jnp.bfloat16)
    top[...] = jnp.full_like(top, -1e30)
    total[...] = jnp.zeros_like(total)
    acc[...] = jnp.zeros_like(acc)

    def attend(chunk, tile):
        at = pl.ds(pl.multiple_of(tile * TILE, TILE), TILE)
        keys = kv[chunk]
        scores = lax.dot_general(
            qs[at], keys, (((1,), (1,)), ((), ())), preferred_element_type=jnp.float32)
        old = top[at][:, :1]
        new = jnp.maximum(old, jnp.max(scores, axis=-1, keepdims=True))
        rescale = jnp.exp2(old - new)
        expanded = jnp.exp2(scores - new)
        parts = expanded[:, 0:128]
        for k in range(1, ROWS // 128):
            parts = parts + expanded[:, k * 128:(k + 1) * 128]
        total[at] = total[at] * rescale + parts
        acc[at] = acc[at] * rescale + jnp.dot(
            expanded.astype(jnp.bfloat16), keys, preferred_element_type=jnp.float32)
        top[at] = jnp.broadcast_to(new, (TILE, 128))

    def attend_all(chunk):
        def one(tile, carry):
            attend(chunk, tile)
            return carry
        lax.fori_loop(0, ROWS // TILE, one, 0)

    attend_all(0)
    for b in range(NB):
        landed(1, b)
    attend_all(1)
    for b in range(NB):
        landed(2 + b, 0)
        push((2 + b, 0), (2 + b, 2), sibling)
        if b < 2:
            push((2 + b, 0), (6, b), right)
        landed(2 + b, 1)
        push((2 + b, 1), (2 + b, 3), sibling)
        if b >= 2:
            push((2 + b, 1), (6, b), left)
        landed(2 + b, 2)
        landed(2 + b, 3)
        attend_all(2 + b)
    for b in range(NB):
        landed(6, b)
        push((6, b), (7, b), sibling)
    attend_all(6)
    for b in range(NB):
        landed(7, b)
    attend_all(7)

    for b in range(NB):
        rows = slice(b * BLK, (b + 1) * BLK)
        whole = jnp.sum(total[rows], axis=-1, keepdims=True)
        mixture = (acc[rows] / whole).astype(jnp.bfloat16)
        attended = jnp.dot(mixture, wv_ref[...], preferred_element_type=jnp.float32).astype(jnp.bfloat16)
        update = jnp.dot(attended, wo_ref[...], preferred_element_type=jnp.float32)
        stage[b] = (rin[b].astype(jnp.float32) + update).astype(jnp.bfloat16)

        @pl.when(remote(b))
        def _(b=b):
            exchange(b, stage, out_ref, r_send, r_recv).start()

        @pl.when(jnp.logical_not(remote(b)))
        def _(b=b):
            out_ref[b] = stage[b]

    for copy in sends:
        copy.wait_send()
    for sends_it, _, copy, _ in rims:
        @pl.when(sends_it)
        def _(copy=copy):
            copy.wait_send()
    for b in range(NB):
        @pl.when(remote(b))
        def _(b=b):
            exchange(b, resid_ref, rin, a_send, a_recv).wait_send()
            exchange(b, stage, out_ref, r_send, r_recv).wait_send()
            arrival(b, out_ref, r_send, r_recv).wait_recv()


def local(
    feats, clip_lengths, norm_gain, conv_weight, conv_bias, attn_gain,
    query_weight, key_weight, value_weight, output_weight,
):
    channels = feats.shape[-1]
    vmem = pl.BlockSpec(memory_space=pltpu.VMEM)
    smem = pl.BlockSpec(memory_space=pltpu.SMEM)
    hbm = pl.BlockSpec(memory_space=pl.ANY)
    dma = pltpu.SemaphoreType.DMA
    half = jax.ShapeDtypeStruct((NB, BLK, channels), jnp.bfloat16)
    resid, mixed = pl.pallas_call(
        block_kernel,
        out_shape=(half, half),
        in_specs=[vmem, smem, vmem, hbm] + [vmem] * 6,
        out_specs=(vmem, vmem),
        scratch_shapes=[
            pltpu.VMEM((3, 3, 3 * channels, channels), jnp.bfloat16),
            pltpu.VMEM((NB + 2, 4, COLS, channels), jnp.bfloat16),
            pltpu.VMEM((NB + 2, 4, COLS, 3 * channels), jnp.bfloat16),
            pltpu.VMEM((NB, BLK, channels), jnp.float32),
            pltpu.VMEM((NB, BLK, channels), jnp.bfloat16),
            pltpu.VMEM((8, ROWS, channels), jnp.bfloat16),
            pltpu.VMEM((ROWS, channels), jnp.bfloat16),
            pltpu.VMEM((ROWS, channels), jnp.float32),
            pltpu.VMEM((ROWS, 128), jnp.float32),
            pltpu.VMEM((ROWS, 128), jnp.float32),
            pltpu.VMEM((NB, BLK, channels), jnp.bfloat16),
            dma((3,)), dma((5,)), dma((5,)), dma((NB,)), dma((NB,)),
            dma((28,)), dma((32,)), dma((NB,)), dma((NB,)),
        ],
        compiler_params=pltpu.CompilerParams(
            collective_id=1, has_side_effects=True, vmem_limit_bytes=56 * 1024 * 1024),
        cost_estimate=pl.CostEstimate(
            flops=16_000_000_000, bytes_accessed=12_000_000, transcendentals=4_000_000),
    )(
        feats, clip_lengths, norm_gain.reshape(1, channels),
        conv_weight.reshape(3, 3, 3 * channels, channels), conv_bias.reshape(1, channels),
        attn_gain.reshape(1, channels), query_weight, key_weight, value_weight, output_weight,
    )
    return resid.reshape(feats.shape), mixed.reshape(feats.shape)


def solution(mesh):
    return jax.shard_map(
        local,
        mesh=mesh,
        in_specs=(P("tm", "space", None, None), P(), P(), P(), P(), P(), P(), P(), P(), P()),
        out_specs=(P("tm", "space", None, None), P("tm", "space", None, None)),
        check_vma=False,
    )
```

```python
import math

import jax
import jax.numpy as jnp
from jax import lax
from jax.experimental import pallas as pl
from jax.experimental.pallas import tpu as pltpu
from jax.sharding import PartitionSpec as P

MESH = pl.DeviceIdType.MESH
COLS = 80
BLK = 2 * COLS
NB = 4
ROWS = NB * BLK
TILE = 320
PLACE = (1, 3, 0, 2)
FRAME = (2, 0, 3, 1)


def scaled(wide, gain):
    mean = jnp.mean(wide * wide, axis=-1, keepdims=True)
    return wide * lax.rsqrt(mean + 1e-06) * gain


def block_kernel(
    clip_ref, norm_gain_ref, bias_ref, gain_ref, feats_hbm, conv_hbm, wq_hbm, wk_hbm, wv_hbm, wo_hbm,
    resid_hbm, out_hbm,
    feats_ref, wq_ref, wk_ref, wv_ref, wo_ref,
    weight, active, taps, conv, resid_ref, rin, kv, qs, acc, top, total, stage,
    f_sem, p_sem, w_sem, o_sem, h_send, h_recv, a_send, a_recv, g_send, g_recv, r_send, r_recv,
):
    tm, space = lax.axis_index("tm"), lax.axis_index("space")
    y, c = tm // 2, tm % 2
    z, x = space // 4, space % 4
    right = (tm, 4 * z + (x + 1) % 4)
    left = (tm, 4 * z + (x + 3) % 4)
    sibling = (2 * y + 1 - c, space)
    slot, core = z % 4, z // 4
    above, below = (space + 31) % 32, (space + 1) % 32
    later, earlier = (tm + 1) % 8, (tm + 7) % 8
    channels = feats_ref.shape[-1]

    home_frame = slot // 2 + 2 * (1 - slot % 2)

    def partner(p):
        return (2 * y + core, 4 * (4 * c + p) + x)

    def remote(p):
        return 4 * c + p != z

    feats_copy = pltpu.make_async_copy(feats_hbm, feats_ref, f_sem)
    feats_copy.start()
    weight_copies = [
        pltpu.make_async_copy(conv_hbm.at[lag], weight.at[lag], w_sem.at[lag]) for lag in range(3)]
    small_copies = [
        pltpu.make_async_copy(source, target, p_sem.at[k])
        for k, (source, target) in enumerate(
            ((wq_hbm, wq_ref), (wk_hbm, wk_ref), (wv_hbm, wv_ref), (wo_hbm, wo_ref)))]
    for copy in weight_copies + small_copies:
        copy.start()

    barrier = pltpu.get_barrier_semaphore()
    for device in (
        left, right, sibling, (tm, above), (tm, below), (later, space), (earlier, space),
    ):
        pl.semaphore_signal(barrier, inc=1, device_id=device, device_id_type=MESH)
    for i in range(NB):
        @pl.when(remote(i))
        def _(i=i):
            pl.semaphore_signal(barrier, inc=1, device_id=partner(i), device_id_type=MESH)

    feats_copy.wait()
    norm_gain = norm_gain_ref[...].reshape(1, channels)
    attn_gain = gain_ref[...].reshape(1, channels)

    def activate(frame):
        for row in range(2):
            unit = scaled(feats_ref[frame, row].astype(jnp.float32), norm_gain)
            active[frame + 2, row + 1] = (unit / (1.0 + jnp.exp(-unit))).astype(jnp.bfloat16)

    for frame in (2, 3):
        activate(frame)

    @pl.when(core == c)
    def _():
        pl.semaphore_wait(barrier, 10)

    @pl.when(core != c)
    def _():
        pl.semaphore_wait(barrier, 11)

    older, recent = pl.ds(2, 2), pl.ds(4, 2)
    first = pl.ds(0, 2)
    has_above, has_below, has_earlier, has_later = space > 0, space < 31, tm > 0, tm < 7

    def rim(k, source, target, device):
        return pltpu.make_async_remote_copy(
            src_ref=active.at[source[0], source[1]], dst_ref=active.at[target[0], target[1]],
            send_sem=h_send.at[k], recv_sem=h_recv.at[k], device_id=device, device_id_type=MESH)

    top_row, low_row, both_rows = pl.ds(1, 1), pl.ds(2, 1), pl.ds(1, 2)
    before_row, after_row = pl.ds(0, 1), pl.ds(3, 1)
    rims = [
        (has_below, has_above, rim(0, (recent, low_row), (recent, before_row), (tm, below)), (recent, before_row)),
        (has_above, has_below, rim(1, (recent, top_row), (recent, after_row), (tm, above)), (recent, after_row)),
        (has_below, has_above, rim(2, (older, low_row), (older, before_row), (tm, below)), (older, before_row)),
        (has_above, has_below, rim(3, (older, top_row), (older, after_row), (tm, above)), (older, after_row)),
        (has_later, has_earlier, rim(4, (recent, both_rows), (first, both_rows), (later, space)), (first, both_rows)),
        (jnp.logical_and(has_later, has_above), jnp.logical_and(has_earlier, has_above),
         rim(5, (recent, before_row), (first, before_row), (later, space)), (first, before_row)),
        (jnp.logical_and(has_later, has_below), jnp.logical_and(has_earlier, has_below),
         rim(6, (recent, after_row), (first, after_row), (later, space)), (first, after_row)),
    ]

    def send_rim(k):
        @pl.when(rims[k][0])
        def _():
            rims[k][2].start()

    for k in (0, 1, 4):
        send_rim(k)
    for frame in (0, 1):
        activate(frame)
    for k in (2, 3):
        send_rim(k)
    for sends_it, gets_it, copy, place in rims:
        @pl.when(jnp.logical_not(gets_it))
        def _(place=place):
            hole = active.at[place[0], place[1]]
            hole[...] = jnp.zeros_like(hole)

    column = lax.broadcasted_iota(jnp.int32, (COLS, channels), 0)

    def spread(frame, row):
        middle = active[frame, row]
        wide = middle.astype(jnp.float32)
        taps[frame, row, :, 0:channels] = jnp.where(
            column == 0, 0.0, pltpu.roll(wide, 1, 0)).astype(jnp.bfloat16)
        taps[frame, row, :, channels:2 * channels] = middle
        taps[frame, row, :, 2 * channels:3 * channels] = jnp.where(
            column == COLS - 1, 0.0, pltpu.roll(wide, COLS - 1, 0)).astype(jnp.bfloat16)

    def product(lag, offset, start, stop):
        window = taps[start + 2 - lag:stop + 2 - lag, offset:offset + 2]
        return jnp.dot(
            window.reshape((stop - start) * BLK, 3 * channels), weight[lag, offset],
            preferred_element_type=jnp.float32)

    lengths = [clip_ref[k] for k in range(3)]
    ends = [lengths[0], lengths[0] + lengths[1], lengths[0] + lengths[1] + lengths[2]]

    def live(frame, lag):
        at = tm * NB + frame
        start = jnp.int32(0)
        for length, end in zip(lengths, ends):
            start = start + jnp.where(end <= at, length, 0)
        return at - lag >= start

    def add(lag, value, start, stop):
        for frame in range(start, stop):
            part = value[(frame - start) * BLK:(frame - start + 1) * BLK]
            if lag:
                part = jnp.where(live(frame, lag), part, 0.0)
            conv[frame] += part

    for frame in (4, 5, 3, 2):
        for row in (1, 2):
            spread(frame, row)
    for frame in range(NB):
        conv[frame] = (
            feats_ref[frame].reshape(BLK, channels).astype(jnp.float32) + bias_ref[...].reshape(1, channels))
    weight_copies[0].wait()
    add(0, product(0, 1, 0, NB), 0, NB)
    for lag in (1, 2):
        weight_copies[lag].wait()
        add(lag, product(lag, 1, 2, NB), 2, NB)

    def received(k):
        gets_it, copy = rims[k][1], rims[k][2]

        @pl.when(gets_it)
        def _():
            copy.wait_recv()

    for k in (0, 1):
        received(k)
        send_rim(k + 5)
    for frame in (4, 5):
        for row in (0, 3):
            spread(frame, row)
    add(0, product(0, 0, 2, NB) + product(0, 2, 2, NB), 2, NB)
    for k in (2, 3):
        received(k)
    for frame in (2, 3):
        for row in (0, 3):
            spread(frame, row)
    for lag in (1, 2):
        add(lag, product(lag, 0, 2, NB) + product(lag, 2, 2, NB), 2, NB)

    def dispatch(i):
        return pltpu.make_async_remote_copy(
            src_ref=resid_ref.at[i], dst_ref=rin.at[slot], send_sem=a_send.at[i],
            recv_sem=a_recv.at[slot], device_id=partner(PLACE[i]), device_id_type=MESH)

    def bring_back(b):
        return pltpu.make_async_remote_copy(
            src_ref=stage.at[b], dst_ref=out_hbm.at[home_frame], send_sem=r_send.at[b],
            recv_sem=r_recv.at[home_frame], device_id=partner(b), device_id_type=MESH)

    def arrival(k, target, recv_sem):
        return pltpu.make_async_remote_copy(
            src_ref=target.at[k], dst_ref=target.at[k], send_sem=a_send.at[k],
            recv_sem=recv_sem.at[k], device_id=sibling, device_id_type=MESH)

    resid_copies = [
        pltpu.make_async_copy(resid_ref.at[i], resid_hbm.at[i], o_sem.at[i]) for i in range(NB)]

    def hand_over(i):
        resid_ref[i] = conv[i].astype(jnp.bfloat16)
        resid_copies[i].start()

        @pl.when(remote(PLACE[i]))
        def _():
            dispatch(i).start()

        @pl.when(jnp.logical_not(remote(PLACE[i])))
        def _():
            rin[PLACE[i]] = resid_ref[i]

    hand_over(2)
    hand_over(3)
    add(0, product(0, 0, 0, 2) + product(0, 2, 0, 2), 0, 2)
    for k in (4, 5, 6):
        received(k)
    for frame in range(2):
        for row in range(4):
            spread(frame, row)
    for lag in (1, 2):
        add(lag, product(lag, 0, 0, 2) + product(lag, 1, 0, 2) + product(lag, 2, 0, 2), 0, 2)
    hand_over(0)
    hand_over(1)

    sends = []

    def block(group, place):
        return kv.at[group, pl.ds(place * BLK, BLK)]

    def push(source, dest, device):
        copy = pltpu.make_async_remote_copy(
            src_ref=block(*source), dst_ref=block(*dest),
            send_sem=g_send.at[len(sends)], recv_sem=g_recv.at[dest[0] * 8 + dest[1]],
            device_id=device, device_id_type=MESH)
        copy.start()
        sends.append(copy)

    def landed(group, place):
        pltpu.make_async_remote_copy(
            src_ref=block(group, place), dst_ref=block(group, place),
            send_sem=g_send.at[0], recv_sem=g_recv.at[group * 8 + place],
            device_id=sibling, device_id_type=MESH).wait_recv()

    home = {0: (1, 0), 2: (1, 1), 1: (2, 0), 3: (2, 1)}

    def normalise(b):
        @pl.when(remote(b))
        def _():
            arrival(b, rin, a_recv).wait_recv()

        kv[0, b * BLK:(b + 1) * BLK] = scaled(rin[b].astype(jnp.float32), attn_gain).astype(jnp.bfloat16)

    for b, other in ((0, 2), (1, 3)):
        normalise(b)
        normalise(other)
        for to_right, to_left in ((b, other), (other, b)):
            group, place = home[to_right]
            push((0, to_right), (group, place), right)
            group, place = home[to_left]
            push((0, to_left), (group, 2 + place), left)
        for own_block in (b, other):
            push((0, own_block), (0, 4 + own_block), sibling)

    for copy in small_copies:
        copy.wait()
    queries = jnp.dot(kv[0, 0:ROWS], wq_ref[...], preferred_element_type=jnp.float32).astype(jnp.bfloat16)
    folded = lax.dot_general(
        queries, wk_ref[...], (((1,), (1,)), ((), ())), preferred_element_type=jnp.float32)
    qs[...] = (folded * (math.log2(math.e) / math.sqrt(folded.shape[-1]))).astype(jnp.bfloat16)
    top[...] = jnp.full_like(top, -1e30)
    total[...] = jnp.zeros_like(total)
    acc[...] = jnp.zeros_like(acc)

    def attend(group, tile, begin=0, end=2 * ROWS):
        at = slice(tile * TILE, (tile + 1) * TILE)
        keys = kv[group, begin:end]
        scores = lax.dot_general(
            qs[at], keys, (((1,), (1,)), ((), ())), preferred_element_type=jnp.float32)
        pieces = [scores[:, k:k + 128] for k in range(0, end - begin, 128)]
        lanes = pieces[0]
        for piece in pieces[1:]:
            lanes = jnp.maximum(lanes, piece)
        old = top[at]
        new = jnp.maximum(old, jnp.broadcast_to(jnp.max(lanes, axis=-1, keepdims=True), old.shape))
        rescale = jnp.exp2(old - new)
        expanded = [jnp.exp2(piece - new) for piece in pieces]
        parts = expanded[0]
        for piece in expanded[1:]:
            parts = parts + piece
        total[at] = total[at] * rescale + parts
        top[at] = new
        weights = jnp.concatenate([piece.astype(jnp.bfloat16) for piece in expanded], axis=1)
        summed = jnp.dot(weights, keys, preferred_element_type=jnp.float32)
        for k in range(0, channels, 128):
            acc[at, k:k + 128] = acc[at, k:k + 128] * rescale + summed[:, k:k + 128]

    tiles = range(ROWS // TILE)
    for b in range(NB):
        landed(0, 4 + b)
    for tile in tiles:
        attend(0, tile)
    for group, from_left, from_right in ((1, 0, 2), (2, 1, 3)):
        for place, forward, device in ((0, from_left, right), (3, from_right, left), (1, None, None), (2, None, None)):
            landed(group, place)
            if forward is not None:
                push((group, place), (3, forward), device)
            push((group, place), (group, 4 + place), sibling)
        for place in range(4):
            landed(group, 4 + place)
        for tile in tiles:
            attend(group, tile)
    for b in (0, 2, 1, 3):
        landed(3, b)
        push((3, b), (3, 4 + b), sibling)
    for tile in tiles:
        attend(3, tile, 0, ROWS)
    for b in range(NB):
        landed(3, 4 + b)

    for tile in tiles:
        attend(3, tile, ROWS, 2 * ROWS)
        at = slice(tile * TILE, (tile + 1) * TILE)
        whole = jnp.sum(total[at], axis=-1, keepdims=True)
        mixture = (acc[at] / whole).astype(jnp.bfloat16)
        attended = jnp.dot(mixture, wv_ref[...], preferred_element_type=jnp.float32).astype(jnp.bfloat16)
        update = jnp.dot(attended, wo_ref[...], preferred_element_type=jnp.float32)
        for half in range(TILE // BLK):
            b = tile * (TILE // BLK) + half
            stage[b] = (
                rin[b].astype(jnp.float32) + update[half * BLK:(half + 1) * BLK]).astype(jnp.bfloat16)

            @pl.when(remote(b))
            def _(b=b):
                bring_back(b).start()

            @pl.when(jnp.logical_not(remote(b)))
            def _(b=b):
                pltpu.make_async_copy(stage.at[b], out_hbm.at[FRAME[b]], o_sem.at[NB]).start()

    for copy in sends:
        copy.wait_send()
    for sends_it, _, copy, _ in rims:
        @pl.when(sends_it)
        def _(copy=copy):
            copy.wait_send()
    for b in range(NB):
        @pl.when(remote(b))
        def _(b=b):
            dispatch(FRAME[b]).wait_send()
            bring_back(b).wait_send()
            arrival(FRAME[b], out_hbm, r_recv).wait_recv()

        @pl.when(jnp.logical_not(remote(b)))
        def _(b=b):
            pltpu.make_async_copy(stage.at[b], out_hbm.at[FRAME[b]], o_sem.at[NB]).wait()
        resid_copies[b].wait()


def finish_kernel(resid_ref, mixed_ref, resid_out, mixed_out, held, in_sems, out_sems):
    pairs = [(resid_ref, resid_out), (mixed_ref, mixed_out)]
    fetched = [pltpu.make_async_copy(pairs[k][0], held.at[k], in_sems.at[k]) for k in range(2)]
    stored = [pltpu.make_async_copy(held.at[k], pairs[k][1], out_sems.at[k]) for k in range(2)]
    for copy in fetched:
        copy.start()
    for first, second in zip(fetched, stored):
        first.wait()
        second.start()
    for copy in stored:
        copy.wait()


def local(
    feats, clip_lengths, norm_gain, conv_weight, conv_bias, attn_gain,
    query_weight, key_weight, value_weight, output_weight,
):
    channels = feats.shape[-1]
    vmem = pl.BlockSpec(memory_space=pltpu.VMEM)
    smem = pl.BlockSpec(memory_space=pltpu.SMEM)
    hbm = pl.BlockSpec(memory_space=pl.ANY)
    dma = pltpu.SemaphoreType.DMA
    half = jax.ShapeDtypeStruct((NB, BLK, channels), jnp.bfloat16)
    resid, mixed = pl.pallas_call(
        block_kernel,
        out_shape=(half, half),
        in_specs=[smem] + [vmem] * 3 + [hbm] * 6,
        out_specs=(hbm, hbm),
        scratch_shapes=[
            pltpu.VMEM(feats.shape, jnp.bfloat16),
        ] + [pltpu.VMEM((channels, channels), jnp.bfloat16)] * 4 + [
            pltpu.VMEM((3, 3, 3 * channels, channels), jnp.bfloat16),
            pltpu.VMEM((NB + 2, 4, COLS, channels), jnp.bfloat16),
            pltpu.VMEM((NB + 2, 4, COLS, 3 * channels), jnp.bfloat16),
            pltpu.VMEM((NB, BLK, channels), jnp.float32),
            pltpu.VMEM((NB, BLK, channels), jnp.bfloat16),
            pltpu.VMEM((NB, BLK, channels), jnp.bfloat16),
            pltpu.VMEM((4, 2 * ROWS, channels), jnp.bfloat16),
            pltpu.VMEM((ROWS, channels), jnp.bfloat16),
            pltpu.VMEM((ROWS, channels), jnp.float32),
            pltpu.VMEM((ROWS, 128), jnp.float32),
            pltpu.VMEM((ROWS, 128), jnp.float32),
            pltpu.VMEM((NB, BLK, channels), jnp.bfloat16),
            dma, dma((4,)), dma((3,)), dma((NB + 1,)), dma((7,)), dma((7,)), dma((NB,)), dma((NB,)),
            dma((28,)), dma((32,)), dma((NB,)), dma((NB,)),
        ],
        compiler_params=pltpu.CompilerParams(
            collective_id=1, has_side_effects=True, vmem_limit_bytes=56 * 1024 * 1024),
        cost_estimate=pl.CostEstimate(
            flops=16_000_000_000, bytes_accessed=12_000_000, transcendentals=4_000_000),
    )(
        clip_lengths, norm_gain, conv_bias, attn_gain, feats,
        conv_weight.reshape(3, 3, 3 * channels, channels),
        query_weight, key_weight, value_weight, output_weight,
    )
    resid, mixed = pl.pallas_call(
        finish_kernel,
        out_shape=(half, half),
        in_specs=[hbm, hbm],
        out_specs=(hbm, hbm),
        scratch_shapes=[pltpu.VMEM((2, NB, BLK, channels), jnp.bfloat16), dma((2,)), dma((2,))],
        compiler_params=pltpu.CompilerParams(vmem_limit_bytes=60 * 1024 * 1024),
    )(resid, mixed)
    return resid.reshape(feats.shape), mixed.reshape(feats.shape)


def solution(mesh):
    return jax.shard_map(
        local,
        mesh=mesh,
        in_specs=(P("tm", "space", None, None), P(), P(), P(), P(), P(), P(), P(), P(), P()),
        out_specs=(P("tm", "space", None, None), P("tm", "space", None, None)),
        check_vma=False,
    )
```

```python
import math

import jax
import jax.numpy as jnp
from jax import lax
from jax.experimental import pallas as pl
from jax.experimental.pallas import tpu as pltpu
from jax.sharding import PartitionSpec as P

MESH = pl.DeviceIdType.MESH
COLS = 80
BLK = 2 * COLS
NB = 4
ROWS = NB * BLK
TILE = 320
PLACE = (1, 3, 0, 2)
FRAME = (2, 0, 3, 1)
TURN = (0, 2, 1, 3)


def scaled(wide, gain):
    mean = jnp.mean(wide * wide, axis=-1, keepdims=True)
    return wide * lax.rsqrt(mean + 1e-06) * gain


def block_kernel(
    clip_ref, norm_gain_ref, bias_ref, gain_ref, feats_hbm, conv_hbm, wq_hbm, wk_hbm, wv_hbm, wo_hbm,
    resid_hbm, out_hbm,
    feats_ref, wq_ref, wk_ref, wv_ref, wo_ref,
    weight, active, taps, conv, resid_ref, rin, kv, qs, acc, top, total, stage,
    f_sem, p_sem, w_sem, o_sem, h_send, h_recv, a_send, a_recv, g_send, g_recv, r_send, r_recv,
):
    tm, space = lax.axis_index("tm"), lax.axis_index("space")
    y, c = tm // 2, tm % 2
    z, x = space // 4, space % 4
    right = (tm, 4 * z + (x + 1) % 4)
    left = (tm, 4 * z + (x + 3) % 4)
    sibling = (2 * y + 1 - c, space)
    slot, core = z % 4, z // 4
    above, below = (space + 31) % 32, (space + 1) % 32
    later, earlier = (tm + 1) % 8, (tm + 7) % 8
    channels = feats_ref.shape[-1]

    home_frame = slot // 2 + 2 * (1 - slot % 2)

    def partner(p):
        return (2 * y + core, 4 * (4 * c + p) + x)

    def remote(p):
        return 4 * c + p != z

    away, step = (core + c) % 2, 1 - 2 * (slot // 2)

    def origin(l):
        turn = TURN[l] + away * (3 - 2 * TURN[l])
        return (slot + step * turn + 8) % 4

    feats_copy = pltpu.make_async_copy(feats_hbm, feats_ref, f_sem)
    feats_copy.start()
    weight_copies = [
        pltpu.make_async_copy(conv_hbm.at[lag], weight.at[lag], w_sem.at[lag]) for lag in range(3)]
    small_copies = [
        pltpu.make_async_copy(source, target, p_sem.at[k])
        for k, (source, target) in enumerate(
            ((wq_hbm, wq_ref), (wk_hbm, wk_ref), (wv_hbm, wv_ref), (wo_hbm, wo_ref)))]
    for copy in weight_copies + small_copies:
        copy.start()

    barrier = pltpu.get_barrier_semaphore()
    for device in (
        left, right, sibling, (tm, above), (tm, below), (later, space), (earlier, space),
    ):
        pl.semaphore_signal(barrier, inc=1, device_id=device, device_id_type=MESH)
    for i in range(NB):
        @pl.when(remote(i))
        def _(i=i):
            pl.semaphore_signal(barrier, inc=1, device_id=partner(i), device_id_type=MESH)

    feats_copy.wait()
    norm_gain = norm_gain_ref[...].reshape(1, channels)
    attn_gain = gain_ref[...].reshape(1, channels)

    def activate(frame):
        for row in range(2):
            unit = scaled(feats_ref[frame, row].astype(jnp.float32), norm_gain)
            active[frame + 2, row + 1] = (unit / (1.0 + jnp.exp(-unit))).astype(jnp.bfloat16)

    for frame in (2, 3):
        activate(frame)

    @pl.when(core == c)
    def _():
        pl.semaphore_wait(barrier, 10)

    @pl.when(core != c)
    def _():
        pl.semaphore_wait(barrier, 11)

    older, recent = pl.ds(2, 2), pl.ds(4, 2)
    first = pl.ds(0, 2)
    has_above, has_below, has_earlier, has_later = space > 0, space < 31, tm > 0, tm < 7

    def rim(k, source, target, device):
        return pltpu.make_async_remote_copy(
            src_ref=active.at[source[0], source[1]], dst_ref=active.at[target[0], target[1]],
            send_sem=h_send.at[k], recv_sem=h_recv.at[k], device_id=device, device_id_type=MESH)

    top_row, low_row, both_rows = pl.ds(1, 1), pl.ds(2, 1), pl.ds(1, 2)
    before_row, after_row = pl.ds(0, 1), pl.ds(3, 1)
    rims = [
        (has_below, has_above, rim(0, (recent, low_row), (recent, before_row), (tm, below)), (recent, before_row)),
        (has_above, has_below, rim(1, (recent, top_row), (recent, after_row), (tm, above)), (recent, after_row)),
        (has_below, has_above, rim(2, (older, low_row), (older, before_row), (tm, below)), (older, before_row)),
        (has_above, has_below, rim(3, (older, top_row), (older, after_row), (tm, above)), (older, after_row)),
        (has_later, has_earlier, rim(4, (recent, both_rows), (first, both_rows), (later, space)), (first, both_rows)),
        (jnp.logical_and(has_later, has_above), jnp.logical_and(has_earlier, has_above),
         rim(5, (recent, before_row), (first, before_row), (later, space)), (first, before_row)),
        (jnp.logical_and(has_later, has_below), jnp.logical_and(has_earlier, has_below),
         rim(6, (recent, after_row), (first, after_row), (later, space)), (first, after_row)),
    ]

    def send_rim(k):
        @pl.when(rims[k][0])
        def _():
            rims[k][2].start()

    for k in (0, 1, 4):
        send_rim(k)
    for frame in (0, 1):
        activate(frame)
    for k in (2, 3):
        send_rim(k)
    for sends_it, gets_it, copy, place in rims:
        @pl.when(jnp.logical_not(gets_it))
        def _(place=place):
            hole = active.at[place[0], place[1]]
            hole[...] = jnp.zeros_like(hole)

    column = lax.broadcasted_iota(jnp.int32, (COLS, channels), 0)

    def spread(frame, row):
        middle = active[frame, row]
        wide = middle.astype(jnp.float32)
        taps[frame, row, :, 0:channels] = jnp.where(
            column == 0, 0.0, pltpu.roll(wide, 1, 0)).astype(jnp.bfloat16)
        taps[frame, row, :, channels:2 * channels] = middle
        taps[frame, row, :, 2 * channels:3 * channels] = jnp.where(
            column == COLS - 1, 0.0, pltpu.roll(wide, COLS - 1, 0)).astype(jnp.bfloat16)

    def product(lag, offset, start, stop):
        window = taps[start + 2 - lag:stop + 2 - lag, offset:offset + 2]
        return jnp.dot(
            window.reshape((stop - start) * BLK, 3 * channels), weight[lag, offset],
            preferred_element_type=jnp.float32)

    lengths = [clip_ref[k] for k in range(3)]
    ends = [lengths[0], lengths[0] + lengths[1], lengths[0] + lengths[1] + lengths[2]]

    def live(frame, lag):
        at = tm * NB + frame
        start = jnp.int32(0)
        for length, end in zip(lengths, ends):
            start = start + jnp.where(end <= at, length, 0)
        return at - lag >= start

    def add(lag, value, start, stop):
        for frame in range(start, stop):
            part = value[(frame - start) * BLK:(frame - start + 1) * BLK]
            if lag:
                part = jnp.where(live(frame, lag), part, 0.0)
            conv[frame] += part

    for frame in (4, 5, 3, 2):
        for row in (1, 2):
            spread(frame, row)
    for frame in range(NB):
        conv[frame] = (
            feats_ref[frame].reshape(BLK, channels).astype(jnp.float32) + bias_ref[...].reshape(1, channels))
    weight_copies[0].wait()
    add(0, product(0, 1, 0, NB), 0, NB)
    for lag in (1, 2):
        weight_copies[lag].wait()
        add(lag, product(lag, 1, 2, NB), 2, NB)

    def received(k):
        gets_it, copy = rims[k][1], rims[k][2]

        @pl.when(gets_it)
        def _():
            copy.wait_recv()

    for k in (0, 1):
        received(k)
        send_rim(k + 5)
    for frame in (4, 5):
        for row in (0, 3):
            spread(frame, row)
    add(0, product(0, 0, 2, NB) + product(0, 2, 2, NB), 2, NB)
    for k in (2, 3):
        received(k)
    for frame in (2, 3):
        for row in (0, 3):
            spread(frame, row)
    for lag in (1, 2):
        add(lag, product(lag, 0, 2, NB) + product(lag, 2, 2, NB), 2, NB)

    def dispatch(i):
        return pltpu.make_async_remote_copy(
            src_ref=resid_ref.at[i], dst_ref=rin.at[slot], send_sem=a_send.at[i],
            recv_sem=a_recv.at[slot], device_id=partner(PLACE[i]), device_id_type=MESH)

    def bring_back(l):
        return pltpu.make_async_remote_copy(
            src_ref=stage.at[l], dst_ref=out_hbm.at[home_frame], send_sem=r_send.at[l],
            recv_sem=r_recv.at[home_frame], device_id=partner(origin(l)), device_id_type=MESH)

    def put_back(l):
        return pltpu.make_async_copy(stage.at[l], out_hbm.at[home_frame], o_sem.at[NB])

    def arrival(k, target, recv_sem):
        return pltpu.make_async_remote_copy(
            src_ref=target.at[k], dst_ref=target.at[k], send_sem=a_send.at[k],
            recv_sem=recv_sem.at[k], device_id=sibling, device_id_type=MESH)

    resid_copies = [
        pltpu.make_async_copy(resid_ref.at[i], resid_hbm.at[i], o_sem.at[i]) for i in range(NB)]

    def hand_over(i):
        resid_ref[i] = conv[i].astype(jnp.bfloat16)
        resid_copies[i].start()

        @pl.when(remote(PLACE[i]))
        def _():
            dispatch(i).start()

        @pl.when(jnp.logical_not(remote(PLACE[i])))
        def _():
            rin[PLACE[i]] = resid_ref[i]

    hand_over(2)
    hand_over(3)
    add(0, product(0, 0, 0, 2) + product(0, 2, 0, 2), 0, 2)
    for k in (4, 5, 6):
        received(k)
    for frame in range(2):
        for row in range(4):
            spread(frame, row)
    for lag in (1, 2):
        add(lag, product(lag, 0, 0, 2) + product(lag, 1, 0, 2) + product(lag, 2, 0, 2), 0, 2)
    hand_over(0)
    hand_over(1)

    sends = []

    def block(group, place):
        return kv.at[group, pl.ds(place * BLK, BLK)]

    def push(source, dest, device):
        copy = pltpu.make_async_remote_copy(
            src_ref=block(*source), dst_ref=block(*dest),
            send_sem=g_send.at[len(sends)], recv_sem=g_recv.at[dest[0] * 8 + dest[1]],
            device_id=device, device_id_type=MESH)
        copy.start()
        sends.append(copy)

    def landed(group, place):
        pltpu.make_async_remote_copy(
            src_ref=block(group, place), dst_ref=block(group, place),
            send_sem=g_send.at[0], recv_sem=g_recv.at[group * 8 + place],
            device_id=sibling, device_id_type=MESH).wait_recv()

    home = {0: (1, 0), 2: (1, 1), 1: (2, 0), 3: (2, 1)}

    def normalise(l):
        b = origin(l)

        @pl.when(remote(b))
        def _():
            arrival(b, rin, a_recv).wait_recv()

        kv[0, l * BLK:(l + 1) * BLK] = scaled(rin[b].astype(jnp.float32), attn_gain).astype(jnp.bfloat16)
        group, place = home[l]
        push((0, l), (group, place), right)
        push((0, l), (group, 2 + place), left)
        push((0, l), (0, 4 + l), sibling)

    for l in TURN:
        normalise(l)

    for copy in small_copies:
        copy.wait()
    queries = jnp.dot(kv[0, 0:ROWS], wq_ref[...], preferred_element_type=jnp.float32).astype(jnp.bfloat16)
    folded = lax.dot_general(
        queries, wk_ref[...], (((1,), (1,)), ((), ())), preferred_element_type=jnp.float32)
    qs[...] = (folded * (math.log2(math.e) / math.sqrt(folded.shape[-1]))).astype(jnp.bfloat16)
    top[...] = jnp.full_like(top, -1e30)
    total[...] = jnp.zeros_like(total)
    acc[...] = jnp.zeros_like(acc)

    def attend(group, tile, begin=0, end=2 * ROWS):
        at = slice(tile * TILE, (tile + 1) * TILE)
        keys = kv[group, begin:end]
        scores = lax.dot_general(
            qs[at], keys, (((1,), (1,)), ((), ())), preferred_element_type=jnp.float32)
        pieces = [scores[:, k:k + 128] for k in range(0, end - begin, 128)]
        lanes = pieces[0]
        for piece in pieces[1:]:
            lanes = jnp.maximum(lanes, piece)
        old = top[at]
        new = jnp.maximum(old, jnp.broadcast_to(jnp.max(lanes, axis=-1, keepdims=True), old.shape))
        rescale = jnp.exp2(old - new)
        expanded = [jnp.exp2(piece - new) for piece in pieces]
        parts = expanded[0]
        for piece in expanded[1:]:
            parts = parts + piece
        total[at] = total[at] * rescale + parts
        top[at] = new
        weights = jnp.concatenate([piece.astype(jnp.bfloat16) for piece in expanded], axis=1)
        summed = jnp.dot(weights, keys, preferred_element_type=jnp.float32)
        for k in range(0, channels, 128):
            acc[at, k:k + 128] = acc[at, k:k + 128] * rescale + summed[:, k:k + 128]

    tiles = range(ROWS // TILE)
    for b in range(NB):
        landed(0, 4 + b)
    for tile in tiles:
        attend(0, tile)
    for group, from_left, from_right in ((1, 0, 2), (2, 1, 3)):
        for place, forward, device in ((0, from_left, right), (3, from_right, left), (1, None, None), (2, None, None)):
            landed(group, place)
            if forward is not None:
                push((group, place), (3, forward), device)
            push((group, place), (group, 4 + place), sibling)
        for place in range(4):
            landed(group, 4 + place)
        for tile in tiles:
            attend(group, tile)
    for b in (0, 2, 1, 3):
        landed(3, b)
        push((3, b), (3, 4 + b), sibling)
    for tile in tiles:
        attend(3, tile, 0, ROWS)
    for b in range(NB):
        landed(3, 4 + b)

    for tile in tiles:
        attend(3, tile, ROWS, 2 * ROWS)
        at = slice(tile * TILE, (tile + 1) * TILE)
        whole = jnp.sum(total[at], axis=-1, keepdims=True)
        mixture = (acc[at] / whole).astype(jnp.bfloat16)
        attended = jnp.dot(mixture, wv_ref[...], preferred_element_type=jnp.float32).astype(jnp.bfloat16)
        update = jnp.dot(attended, wo_ref[...], preferred_element_type=jnp.float32)
        for half in range(TILE // BLK):
            l = tile * (TILE // BLK) + half
            stage[l] = (
                rin[origin(l)].astype(jnp.float32) + update[half * BLK:(half + 1) * BLK]).astype(jnp.bfloat16)

            @pl.when(remote(origin(l)))
            def _(l=l):
                bring_back(l).start()

            @pl.when(jnp.logical_not(remote(origin(l))))
            def _(l=l):
                put_back(l).start()

    for copy in sends:
        copy.wait_send()
    for sends_it, _, copy, _ in rims:
        @pl.when(sends_it)
        def _(copy=copy):
            copy.wait_send()
    for b in range(NB):
        @pl.when(remote(b))
        def _(b=b):
            dispatch(FRAME[b]).wait_send()
            arrival(FRAME[b], out_hbm, r_recv).wait_recv()

        @pl.when(remote(origin(b)))
        def _(b=b):
            bring_back(b).wait_send()

        @pl.when(jnp.logical_not(remote(origin(b))))
        def _(b=b):
            put_back(b).wait()
        resid_copies[b].wait()


def finish_kernel(resid_ref, mixed_ref, resid_out, mixed_out, held, in_sems, out_sems):
    pairs = [(resid_ref, resid_out), (mixed_ref, mixed_out)]
    fetched = [pltpu.make_async_copy(pairs[k][0], held.at[k], in_sems.at[k]) for k in range(2)]
    stored = [pltpu.make_async_copy(held.at[k], pairs[k][1], out_sems.at[k]) for k in range(2)]
    for copy in fetched:
        copy.start()
    for first, second in zip(fetched, stored):
        first.wait()
        second.start()
    for copy in stored:
        copy.wait()


def local(
    feats, clip_lengths, norm_gain, conv_weight, conv_bias, attn_gain,
    query_weight, key_weight, value_weight, output_weight,
):
    channels = feats.shape[-1]
    vmem = pl.BlockSpec(memory_space=pltpu.VMEM)
    smem = pl.BlockSpec(memory_space=pltpu.SMEM)
    hbm = pl.BlockSpec(memory_space=pl.ANY)
    dma = pltpu.SemaphoreType.DMA
    half = jax.ShapeDtypeStruct((NB, BLK, channels), jnp.bfloat16)
    resid, mixed = pl.pallas_call(
        block_kernel,
        out_shape=(half, half),
        in_specs=[smem] + [vmem] * 3 + [hbm] * 6,
        out_specs=(hbm, hbm),
        scratch_shapes=[
            pltpu.VMEM(feats.shape, jnp.bfloat16),
        ] + [pltpu.VMEM((channels, channels), jnp.bfloat16)] * 4 + [
            pltpu.VMEM((3, 3, 3 * channels, channels), jnp.bfloat16),
            pltpu.VMEM((NB + 2, 4, COLS, channels), jnp.bfloat16),
            pltpu.VMEM((NB + 2, 4, COLS, 3 * channels), jnp.bfloat16),
            pltpu.VMEM((NB, BLK, channels), jnp.float32),
            pltpu.VMEM((NB, BLK, channels), jnp.bfloat16),
            pltpu.VMEM((NB, BLK, channels), jnp.bfloat16),
            pltpu.VMEM((4, 2 * ROWS, channels), jnp.bfloat16),
            pltpu.VMEM((ROWS, channels), jnp.bfloat16),
            pltpu.VMEM((ROWS, channels), jnp.float32),
            pltpu.VMEM((ROWS, 128), jnp.float32),
            pltpu.VMEM((ROWS, 128), jnp.float32),
            pltpu.VMEM((NB, BLK, channels), jnp.bfloat16),
            dma, dma((4,)), dma((3,)), dma((NB + 1,)), dma((7,)), dma((7,)), dma((NB,)), dma((NB,)),
            dma((28,)), dma((32,)), dma((NB,)), dma((NB,)),
        ],
        compiler_params=pltpu.CompilerParams(
            collective_id=1, has_side_effects=True, vmem_limit_bytes=56 * 1024 * 1024),
        cost_estimate=pl.CostEstimate(
            flops=16_000_000_000, bytes_accessed=12_000_000, transcendentals=4_000_000),
    )(
        clip_lengths, norm_gain, conv_bias, attn_gain, feats,
        conv_weight.reshape(3, 3, 3 * channels, channels),
        query_weight, key_weight, value_weight, output_weight,
    )
    resid, mixed = pl.pallas_call(
        finish_kernel,
        out_shape=(half, half),
        in_specs=[hbm, hbm],
        out_specs=(hbm, hbm),
        scratch_shapes=[pltpu.VMEM((2, NB, BLK, channels), jnp.bfloat16), dma((2,)), dma((2,))],
        compiler_params=pltpu.CompilerParams(vmem_limit_bytes=60 * 1024 * 1024),
    )(resid, mixed)
    return resid.reshape(feats.shape), mixed.reshape(feats.shape)


def solution(mesh):
    return jax.shard_map(
        local,
        mesh=mesh,
        in_specs=(P("tm", "space", None, None), P(), P(), P(), P(), P(), P(), P(), P(), P()),
        out_specs=(P("tm", "space", None, None), P("tm", "space", None, None)),
        check_vma=False,
    )
```

```python
import math

import jax
import jax.numpy as jnp
from jax import lax
from jax.experimental import pallas as pl
from jax.experimental.pallas import tpu as pltpu
from jax.sharding import PartitionSpec as P

MESH = pl.DeviceIdType.MESH
COLS = 80
BLK = 2 * COLS
NB = 4
ROWS = NB * BLK
TILE = 320
FRAME = (2, 0, 3, 1)
TURN = (0, 2, 1, 3)


def scaled(wide, gain):
    mean = jnp.mean(wide * wide, axis=-1, keepdims=True)
    return wide * lax.rsqrt(mean + 1e-06) * gain


def block_kernel(
    clip_ref, norm_gain_ref, bias_ref, gain_ref, feats_hbm, conv_hbm, wq_hbm, wk_hbm, wv_hbm, wo_hbm,
    resid_hbm, out_hbm,
    feats_ref, wq_ref, wk_ref, wv_ref, wo_ref,
    weight, active, taps, conv, resid_ref, rin, kv, qs, acc, top, total, stage,
    f_sem, p_sem, w_sem, o_sem, h_send, h_recv, a_send, a_recv, g_send, g_recv, r_send, r_recv,
):
    tm, space = lax.axis_index("tm"), lax.axis_index("space")
    y, c = tm // 2, tm % 2
    z, x = space // 4, space % 4
    right = (tm, 4 * z + (x + 1) % 4)
    left = (tm, 4 * z + (x + 3) % 4)
    sibling = (2 * y + 1 - c, space)
    slot, core = z % 4, z // 4
    above, below = (space + 31) % 32, (space + 1) % 32
    later, earlier = (tm + 1) % 8, (tm + 7) % 8
    channels = feats_ref.shape[-1]

    home_frame = slot // 2 + 2 * (1 - slot % 2)

    def partner(p):
        return (2 * y + core, 4 * (4 * c + p) + x)

    def remote(p):
        return 4 * c + p != z

    away, odd, high = (core + c) % 2, slot % 2, slot // 2
    near = (high + away) % 2
    first_near = (1 - away) * odd + away * (1 - high)
    first_far = (1 - away) * high + away * (1 - odd)
    order = (
        2 * near + first_near, 2 * near + 1 - first_near,
        2 * (1 - near) + first_far, 2 * (1 - near) + 1 - first_far)

    def origin(l):
        return order[TURN[l]]

    feats_copy = pltpu.make_async_copy(feats_hbm, feats_ref, f_sem)
    feats_copy.start()
    weight_copies = [
        pltpu.make_async_copy(conv_hbm.at[lag], weight.at[lag], w_sem.at[lag]) for lag in range(3)]
    small_copies = [
        pltpu.make_async_copy(source, target, p_sem.at[k])
        for k, (source, target) in enumerate(
            ((wq_hbm, wq_ref), (wk_hbm, wk_ref), (wv_hbm, wv_ref), (wo_hbm, wo_ref)))]
    for copy in weight_copies + small_copies:
        copy.start()

    barrier = pltpu.get_barrier_semaphore()
    for device in (
        left, right, sibling, (tm, above), (tm, below), (later, space), (earlier, space),
    ):
        pl.semaphore_signal(barrier, inc=1, device_id=device, device_id_type=MESH)
    for i in range(NB):
        @pl.when(remote(i))
        def _(i=i):
            pl.semaphore_signal(barrier, inc=1, device_id=partner(i), device_id_type=MESH)

    feats_copy.wait()
    norm_gain = norm_gain_ref[...].reshape(1, channels)
    attn_gain = gain_ref[...].reshape(1, channels)

    def activate(frame):
        for row in range(2):
            unit = scaled(feats_ref[frame, row].astype(jnp.float32), norm_gain)
            active[frame + 2, row + 1] = (unit / (1.0 + jnp.exp(-unit))).astype(jnp.bfloat16)

    for frame in (2, 3):
        activate(frame)

    @pl.when(core == c)
    def _():
        pl.semaphore_wait(barrier, 10)

    @pl.when(core != c)
    def _():
        pl.semaphore_wait(barrier, 11)

    older, recent = pl.ds(2, 2), pl.ds(4, 2)
    first = pl.ds(0, 2)
    has_above, has_below, has_earlier, has_later = space > 0, space < 31, tm > 0, tm < 7

    def rim(k, source, target, device):
        return pltpu.make_async_remote_copy(
            src_ref=active.at[source[0], source[1]], dst_ref=active.at[target[0], target[1]],
            send_sem=h_send.at[k], recv_sem=h_recv.at[k], device_id=device, device_id_type=MESH)

    top_row, low_row, both_rows = pl.ds(1, 1), pl.ds(2, 1), pl.ds(1, 2)
    before_row, after_row = pl.ds(0, 1), pl.ds(3, 1)
    rims = [
        (has_below, has_above, rim(0, (recent, low_row), (recent, before_row), (tm, below)), (recent, before_row)),
        (has_above, has_below, rim(1, (recent, top_row), (recent, after_row), (tm, above)), (recent, after_row)),
        (has_below, has_above, rim(2, (older, low_row), (older, before_row), (tm, below)), (older, before_row)),
        (has_above, has_below, rim(3, (older, top_row), (older, after_row), (tm, above)), (older, after_row)),
        (has_later, has_earlier, rim(4, (recent, both_rows), (first, both_rows), (later, space)), (first, both_rows)),
        (jnp.logical_and(has_later, has_above), jnp.logical_and(has_earlier, has_above),
         rim(5, (recent, before_row), (first, before_row), (later, space)), (first, before_row)),
        (jnp.logical_and(has_later, has_below), jnp.logical_and(has_earlier, has_below),
         rim(6, (recent, after_row), (first, after_row), (later, space)), (first, after_row)),
    ]

    def send_rim(k):
        @pl.when(rims[k][0])
        def _():
            rims[k][2].start()

    for k in (0, 1, 4):
        send_rim(k)
    for frame in (0, 1):
        activate(frame)
    for k in (2, 3):
        send_rim(k)
    for sends_it, gets_it, copy, place in rims:
        @pl.when(jnp.logical_not(gets_it))
        def _(place=place):
            hole = active.at[place[0], place[1]]
            hole[...] = jnp.zeros_like(hole)

    column = lax.broadcasted_iota(jnp.int32, (COLS, channels), 0)

    def spread(frame, row):
        middle = active[frame, row]
        wide = middle.astype(jnp.float32)
        taps[frame, row, :, 0:channels] = jnp.where(
            column == 0, 0.0, pltpu.roll(wide, 1, 0)).astype(jnp.bfloat16)
        taps[frame, row, :, channels:2 * channels] = middle
        taps[frame, row, :, 2 * channels:3 * channels] = jnp.where(
            column == COLS - 1, 0.0, pltpu.roll(wide, COLS - 1, 0)).astype(jnp.bfloat16)

    def product(lag, offset, start, stop):
        window = taps[start + 2 - lag:stop + 2 - lag, offset:offset + 2]
        return jnp.dot(
            window.reshape((stop - start) * BLK, 3 * channels), weight[lag, offset],
            preferred_element_type=jnp.float32)

    lengths = [clip_ref[k] for k in range(3)]
    ends = [lengths[0], lengths[0] + lengths[1], lengths[0] + lengths[1] + lengths[2]]

    def live(frame, lag):
        at = tm * NB + frame
        start = jnp.int32(0)
        for length, end in zip(lengths, ends):
            start = start + jnp.where(end <= at, length, 0)
        return at - lag >= start

    def add(lag, value, start, stop):
        for frame in range(start, stop):
            part = value[(frame - start) * BLK:(frame - start + 1) * BLK]
            if lag:
                part = jnp.where(live(frame, lag), part, 0.0)
            conv[frame] += part

    for frame in (4, 5, 3, 2):
        for row in (1, 2):
            spread(frame, row)
    for frame in range(NB):
        conv[frame] = (
            feats_ref[frame].reshape(BLK, channels).astype(jnp.float32) + bias_ref[...].reshape(1, channels))
    weight_copies[0].wait()
    add(0, product(0, 1, 0, NB), 0, NB)
    for lag in (1, 2):
        weight_copies[lag].wait()
        add(lag, product(lag, 1, 2, NB), 2, NB)

    def received(k):
        gets_it, copy = rims[k][1], rims[k][2]

        @pl.when(gets_it)
        def _():
            copy.wait_recv()

    for k in (0, 1):
        received(k)
        send_rim(k + 5)
    for frame in (4, 5):
        for row in (0, 3):
            spread(frame, row)
    add(0, product(0, 0, 2, NB) + product(0, 2, 2, NB), 2, NB)
    for k in (2, 3):
        received(k)
    for frame in (2, 3):
        for row in (0, 3):
            spread(frame, row)
    for lag in (1, 2):
        add(lag, product(lag, 0, 2, NB) + product(lag, 2, 2, NB), 2, NB)

    def dispatch(i, p):
        return pltpu.make_async_remote_copy(
            src_ref=resid_ref.at[i], dst_ref=rin.at[slot], send_sem=a_send.at[i],
            recv_sem=a_recv.at[slot], device_id=partner(p), device_id_type=MESH)

    def bring_back(l):
        return pltpu.make_async_remote_copy(
            src_ref=stage.at[l], dst_ref=out_hbm.at[home_frame], send_sem=r_send.at[l],
            recv_sem=r_recv.at[home_frame], device_id=partner(origin(l)), device_id_type=MESH)

    def put_back(l):
        return pltpu.make_async_copy(stage.at[l], out_hbm.at[home_frame], o_sem.at[NB])

    def arrival(k, target, recv_sem):
        return pltpu.make_async_remote_copy(
            src_ref=target.at[k], dst_ref=target.at[k], send_sem=a_send.at[k],
            recv_sem=recv_sem.at[k], device_id=sibling, device_id_type=MESH)

    resid_copies = [
        pltpu.make_async_copy(resid_ref.at[i], resid_hbm.at[i], o_sem.at[i]) for i in range(NB)]

    def settle(i):
        resid_ref[i] = conv[i].astype(jnp.bfloat16)
        resid_copies[i].start()

    def hand_over(i, p):
        @pl.when(remote(p))
        def _():
            dispatch(i, p).start()

        @pl.when(jnp.logical_not(remote(p)))
        def _():
            rin[slot] = resid_ref[i]

    for i in (2, 3):
        settle(i)
    hand_over(2 + near, 2 * near)
    add(0, product(0, 0, 0, 2) + product(0, 2, 0, 2), 0, 2)
    hand_over(3 - near, 2 - 2 * near)
    for k in (4, 5, 6):
        received(k)
    for frame in range(2):
        for row in range(4):
            spread(frame, row)
    for lag in (1, 2):
        add(lag, product(lag, 0, 0, 2) + product(lag, 1, 0, 2) + product(lag, 2, 0, 2), 0, 2)
    for i in (0, 1):
        settle(i)
    hand_over(near, 1 + 2 * near)

    sends = []

    def block(group, place):
        return kv.at[group, pl.ds(place * BLK, BLK)]

    def push(source, dest, device):
        copy = pltpu.make_async_remote_copy(
            src_ref=block(*source), dst_ref=block(*dest),
            send_sem=g_send.at[len(sends)], recv_sem=g_recv.at[dest[0] * 8 + dest[1]],
            device_id=device, device_id_type=MESH)
        copy.start()
        sends.append(copy)

    def landed(group, place):
        pltpu.make_async_remote_copy(
            src_ref=block(group, place), dst_ref=block(group, place),
            send_sem=g_send.at[0], recv_sem=g_recv.at[group * 8 + place],
            device_id=sibling, device_id_type=MESH).wait_recv()

    home = {0: (1, 0), 2: (1, 1), 1: (2, 0), 3: (2, 1)}

    def normalise(l):
        b = origin(l)

        @pl.when(remote(b))
        def _():
            arrival(b, rin, a_recv).wait_recv()

        kv[0, l * BLK:(l + 1) * BLK] = scaled(rin[b].astype(jnp.float32), attn_gain).astype(jnp.bfloat16)
        group, place = home[l]
        push((0, l), (group, place), right)
        push((0, l), (group, 2 + place), left)
        push((0, l), (0, 4 + l), sibling)

    for l in (0, 2):
        normalise(l)

    @pl.when(remote(1 + 2 * near))
    def _():
        dispatch(near, 1 + 2 * near).wait_send()

    hand_over(1 - near, 3 - 2 * near)
    for l in (1, 3):
        normalise(l)

    for copy in small_copies:
        copy.wait()
    queries = jnp.dot(kv[0, 0:ROWS], wq_ref[...], preferred_element_type=jnp.float32).astype(jnp.bfloat16)
    folded = lax.dot_general(
        queries, wk_ref[...], (((1,), (1,)), ((), ())), preferred_element_type=jnp.float32)
    qs[...] = (folded * (math.log2(math.e) / math.sqrt(folded.shape[-1]))).astype(jnp.bfloat16)
    top[...] = jnp.full_like(top, -1e30)
    total[...] = jnp.zeros_like(total)
    acc[...] = jnp.zeros_like(acc)

    def attend(group, tile, begin=0, end=2 * ROWS):
        at = slice(tile * TILE, (tile + 1) * TILE)
        keys = kv[group, begin:end]
        scores = lax.dot_general(
            qs[at], keys, (((1,), (1,)), ((), ())), preferred_element_type=jnp.float32)
        pieces = [scores[:, k:k + 128] for k in range(0, end - begin, 128)]
        lanes = pieces[0]
        for piece in pieces[1:]:
            lanes = jnp.maximum(lanes, piece)
        old = top[at]
        new = jnp.maximum(old, jnp.broadcast_to(jnp.max(lanes, axis=-1, keepdims=True), old.shape))
        rescale = jnp.exp2(old - new)
        expanded = [jnp.exp2(piece - new) for piece in pieces]
        parts = expanded[0]
        for piece in expanded[1:]:
            parts = parts + piece
        total[at] = total[at] * rescale + parts
        top[at] = new
        weights = jnp.concatenate([piece.astype(jnp.bfloat16) for piece in expanded], axis=1)
        summed = jnp.dot(weights, keys, preferred_element_type=jnp.float32)
        for k in range(0, channels, 128):
            acc[at, k:k + 128] = acc[at, k:k + 128] * rescale + summed[:, k:k + 128]

    tiles = range(ROWS // TILE)

    def relay(group, from_left, from_right):
        for place, forward, device in ((0, from_left, right), (3, from_right, left), (1, None, None), (2, None, None)):
            landed(group, place)
            if forward is not None:
                push((group, place), (3, forward), device)
            push((group, place), (group, 4 + place), sibling)

    relay(1, 0, 2)
    for b in range(NB):
        landed(0, 4 + b)
    for tile in tiles:
        attend(0, tile)
    for place in range(4):
        landed(1, 4 + place)
    for tile in tiles:
        attend(1, tile)
    relay(2, 1, 3)
    for place in range(4):
        landed(2, 4 + place)
    for tile in tiles:
        attend(2, tile)
    for b in (0, 2, 1, 3):
        landed(3, b)
        push((3, b), (3, 4 + b), sibling)
    for tile in tiles:
        attend(3, tile, 0, ROWS)
    for b in range(NB):
        landed(3, 4 + b)

    for tile in tiles:
        attend(3, tile, ROWS, 2 * ROWS)
        at = slice(tile * TILE, (tile + 1) * TILE)
        whole = jnp.sum(total[at], axis=-1, keepdims=True)
        mixture = (acc[at] / whole).astype(jnp.bfloat16)
        attended = jnp.dot(mixture, wv_ref[...], preferred_element_type=jnp.float32).astype(jnp.bfloat16)
        update = jnp.dot(attended, wo_ref[...], preferred_element_type=jnp.float32)
        for half in range(TILE // BLK):
            l = tile * (TILE // BLK) + half
            stage[l] = (
                rin[origin(l)].astype(jnp.float32) + update[half * BLK:(half + 1) * BLK]).astype(jnp.bfloat16)

            @pl.when(remote(origin(l)))
            def _(l=l):
                bring_back(l).start()

            @pl.when(jnp.logical_not(remote(origin(l))))
            def _(l=l):
                put_back(l).start()

    for copy in sends:
        copy.wait_send()
    for sends_it, _, copy, _ in rims:
        @pl.when(sends_it)
        def _(copy=copy):
            copy.wait_send()
    for i, p in ((2 + near, 2 * near), (3 - near, 2 - 2 * near), (1 - near, 3 - 2 * near)):
        @pl.when(remote(p))
        def _(i=i, p=p):
            dispatch(i, p).wait_send()
    for b in range(NB):
        @pl.when(remote(b))
        def _(b=b):
            arrival(FRAME[b], out_hbm, r_recv).wait_recv()

        @pl.when(remote(origin(b)))
        def _(b=b):
            bring_back(b).wait_send()

        @pl.when(jnp.logical_not(remote(origin(b))))
        def _(b=b):
            put_back(b).wait()
        resid_copies[b].wait()


def finish_kernel(resid_ref, mixed_ref, resid_out, mixed_out, held, in_sems, out_sems):
    pairs = [(resid_ref, resid_out), (mixed_ref, mixed_out)]
    fetched = [pltpu.make_async_copy(pairs[k][0], held.at[k], in_sems.at[k]) for k in range(2)]
    stored = [pltpu.make_async_copy(held.at[k], pairs[k][1], out_sems.at[k]) for k in range(2)]
    for copy in fetched:
        copy.start()
    for first, second in zip(fetched, stored):
        first.wait()
        second.start()
    for copy in stored:
        copy.wait()


def local(
    feats, clip_lengths, norm_gain, conv_weight, conv_bias, attn_gain,
    query_weight, key_weight, value_weight, output_weight,
):
    channels = feats.shape[-1]
    vmem = pl.BlockSpec(memory_space=pltpu.VMEM)
    smem = pl.BlockSpec(memory_space=pltpu.SMEM)
    hbm = pl.BlockSpec(memory_space=pl.ANY)
    dma = pltpu.SemaphoreType.DMA
    half = jax.ShapeDtypeStruct((NB, BLK, channels), jnp.bfloat16)
    resid, mixed = pl.pallas_call(
        block_kernel,
        out_shape=(half, half),
        in_specs=[smem] + [vmem] * 3 + [hbm] * 6,
        out_specs=(hbm, hbm),
        scratch_shapes=[
            pltpu.VMEM(feats.shape, jnp.bfloat16),
        ] + [pltpu.VMEM((channels, channels), jnp.bfloat16)] * 4 + [
            pltpu.VMEM((3, 3, 3 * channels, channels), jnp.bfloat16),
            pltpu.VMEM((NB + 2, 4, COLS, channels), jnp.bfloat16),
            pltpu.VMEM((NB + 2, 4, COLS, 3 * channels), jnp.bfloat16),
            pltpu.VMEM((NB, BLK, channels), jnp.float32),
            pltpu.VMEM((NB, BLK, channels), jnp.bfloat16),
            pltpu.VMEM((NB, BLK, channels), jnp.bfloat16),
            pltpu.VMEM((4, 2 * ROWS, channels), jnp.bfloat16),
            pltpu.VMEM((ROWS, channels), jnp.bfloat16),
            pltpu.VMEM((ROWS, channels), jnp.float32),
            pltpu.VMEM((ROWS, 128), jnp.float32),
            pltpu.VMEM((ROWS, 128), jnp.float32),
            pltpu.VMEM((NB, BLK, channels), jnp.bfloat16),
            dma, dma((4,)), dma((3,)), dma((NB + 1,)), dma((7,)), dma((7,)), dma((NB,)), dma((NB,)),
            dma((28,)), dma((32,)), dma((NB,)), dma((NB,)),
        ],
        compiler_params=pltpu.CompilerParams(
            collective_id=1, has_side_effects=True, vmem_limit_bytes=56 * 1024 * 1024),
        cost_estimate=pl.CostEstimate(
            flops=16_000_000_000, bytes_accessed=12_000_000, transcendentals=4_000_000),
    )(
        clip_lengths, norm_gain, conv_bias, attn_gain, feats,
        conv_weight.reshape(3, 3, 3 * channels, channels),
        query_weight, key_weight, value_weight, output_weight,
    )
    resid, mixed = pl.pallas_call(
        finish_kernel,
        out_shape=(half, half),
        in_specs=[hbm, hbm],
        out_specs=(hbm, hbm),
        scratch_shapes=[pltpu.VMEM((2, NB, BLK, channels), jnp.bfloat16), dma((2,)), dma((2,))],
        compiler_params=pltpu.CompilerParams(vmem_limit_bytes=60 * 1024 * 1024),
    )(resid, mixed)
    return resid.reshape(feats.shape), mixed.reshape(feats.shape)


def solution(mesh):
    return jax.shard_map(
        local,
        mesh=mesh,
        in_specs=(P("tm", "space", None, None), P(), P(), P(), P(), P(), P(), P(), P(), P()),
        out_specs=(P("tm", "space", None, None), P("tm", "space", None, None)),
        check_vma=False,
    )
```

```python
import math

import jax
import jax.numpy as jnp
from jax import lax
from jax.experimental import pallas as pl
from jax.experimental.pallas import tpu as pltpu
from jax.sharding import PartitionSpec as P

MESH = pl.DeviceIdType.MESH
COLS = 80
BLK = 2 * COLS
NB = 4
ROWS = NB * BLK
TILE = 320
PLACE = (1, 3, 0, 2)
FRAME = (2, 0, 3, 1)
TURN = (0, 2, 1, 3)


def scaled(wide, gain):
    mean = jnp.mean(wide * wide, axis=-1, keepdims=True)
    return wide * lax.rsqrt(mean + 1e-06) * gain


def block_kernel(
    clip_ref, norm_gain_ref, bias_ref, gain_ref, feats_hbm, conv_hbm, wq_hbm, wk_hbm, wv_hbm, wo_hbm,
    resid_hbm, out_hbm,
    feats_ref, wq_ref, wk_ref, wv_ref, wo_ref,
    weight, active, taps, conv, resid_ref, rin, kv, qs, acc, top, total, stage,
    f_sem, p_sem, w_sem, o_sem, h_send, h_recv, a_send, a_recv, g_send, g_recv, r_send, r_recv,
):
    tm, space = lax.axis_index("tm"), lax.axis_index("space")
    y, c = tm // 2, tm % 2
    z, x = space // 4, space % 4
    right = (tm, 4 * z + (x + 1) % 4)
    left = (tm, 4 * z + (x + 3) % 4)
    sibling = (2 * y + 1 - c, space)
    slot, core = z % 4, z // 4
    above, below = (space + 31) % 32, (space + 1) % 32
    later, earlier = (tm + 1) % 8, (tm + 7) % 8
    channels = feats_ref.shape[-1]

    home_frame = slot // 2 + 2 * (1 - slot % 2)

    def partner(p):
        return (2 * y + core, 4 * (4 * c + p) + x)

    def remote(p):
        return 4 * c + p != z

    away, step = (core + c) % 2, 1 - 2 * (slot // 2)

    def origin(l):
        turn = TURN[l] + away * (3 - 2 * TURN[l])
        return (slot + step * turn + 8) % 4

    feats_copy = pltpu.make_async_copy(feats_hbm, feats_ref, f_sem)
    feats_copy.start()
    weight_copies = [
        pltpu.make_async_copy(conv_hbm.at[lag], weight.at[lag], w_sem.at[lag]) for lag in range(3)]
    small_copies = [
        pltpu.make_async_copy(source, target, p_sem.at[k])
        for k, (source, target) in enumerate(
            ((wq_hbm, wq_ref), (wk_hbm, wk_ref), (wv_hbm, wv_ref), (wo_hbm, wo_ref)))]
    for copy in weight_copies + small_copies:
        copy.start()

    barrier = pltpu.get_barrier_semaphore()
    for device in (
        left, right, sibling, (tm, above), (tm, below), (later, space), (earlier, space),
    ):
        pl.semaphore_signal(barrier, inc=1, device_id=device, device_id_type=MESH)
    for i in range(NB):
        @pl.when(remote(i))
        def _(i=i):
            pl.semaphore_signal(barrier, inc=1, device_id=partner(i), device_id_type=MESH)

    feats_copy.wait()
    norm_gain = norm_gain_ref[...].reshape(1, channels)
    attn_gain = gain_ref[...].reshape(1, channels)

    def activate(frame):
        for row in range(2):
            unit = scaled(feats_ref[frame, row].astype(jnp.float32), norm_gain)
            active[frame + 2, row + 1] = (unit / (1.0 + jnp.exp(-unit))).astype(jnp.bfloat16)

    for frame in (2, 3):
        activate(frame)

    @pl.when(core == c)
    def _():
        pl.semaphore_wait(barrier, 10)

    @pl.when(core != c)
    def _():
        pl.semaphore_wait(barrier, 11)

    older, recent = pl.ds(2, 2), pl.ds(4, 2)
    first = pl.ds(0, 2)
    has_above, has_below, has_earlier, has_later = space > 0, space < 31, tm > 0, tm < 7

    def rim(k, source, target, device):
        return pltpu.make_async_remote_copy(
            src_ref=active.at[source[0], source[1]], dst_ref=active.at[target[0], target[1]],
            send_sem=h_send.at[k], recv_sem=h_recv.at[k], device_id=device, device_id_type=MESH)

    top_row, low_row, both_rows = pl.ds(1, 1), pl.ds(2, 1), pl.ds(1, 2)
    before_row, after_row = pl.ds(0, 1), pl.ds(3, 1)
    rims = [
        (has_below, has_above, rim(0, (recent, low_row), (recent, before_row), (tm, below)), (recent, before_row)),
        (has_above, has_below, rim(1, (recent, top_row), (recent, after_row), (tm, above)), (recent, after_row)),
        (has_below, has_above, rim(2, (older, low_row), (older, before_row), (tm, below)), (older, before_row)),
        (has_above, has_below, rim(3, (older, top_row), (older, after_row), (tm, above)), (older, after_row)),
        (has_later, has_earlier, rim(4, (recent, both_rows), (first, both_rows), (later, space)), (first, both_rows)),
        (jnp.logical_and(has_later, has_above), jnp.logical_and(has_earlier, has_above),
         rim(5, (recent, before_row), (first, before_row), (later, space)), (first, before_row)),
        (jnp.logical_and(has_later, has_below), jnp.logical_and(has_earlier, has_below),
         rim(6, (recent, after_row), (first, after_row), (later, space)), (first, after_row)),
    ]

    def send_rim(k):
        @pl.when(rims[k][0])
        def _():
            rims[k][2].start()

    for k in (0, 1, 4):
        send_rim(k)
    for frame in (0, 1):
        activate(frame)
    for k in (2, 3):
        send_rim(k)
    for sends_it, gets_it, copy, place in rims:
        @pl.when(jnp.logical_not(gets_it))
        def _(place=place):
            hole = active.at[place[0], place[1]]
            hole[...] = jnp.zeros_like(hole)

    column = lax.broadcasted_iota(jnp.int32, (COLS, channels), 0)

    def spread(frame, row):
        middle = active[frame, row]
        wide = middle.astype(jnp.float32)
        taps[frame, row, :, 0:channels] = jnp.where(
            column == 0, 0.0, pltpu.roll(wide, 1, 0)).astype(jnp.bfloat16)
        taps[frame, row, :, channels:2 * channels] = middle
        taps[frame, row, :, 2 * channels:3 * channels] = jnp.where(
            column == COLS - 1, 0.0, pltpu.roll(wide, COLS - 1, 0)).astype(jnp.bfloat16)

    def product(lag, offset, start, stop):
        window = taps[start + 2 - lag:stop + 2 - lag, offset:offset + 2]
        return jnp.dot(
            window.reshape((stop - start) * BLK, 3 * channels), weight[lag, offset],
            preferred_element_type=jnp.float32)

    lengths = [clip_ref[k] for k in range(3)]
    ends = [lengths[0], lengths[0] + lengths[1], lengths[0] + lengths[1] + lengths[2]]

    def live(frame, lag):
        at = tm * NB + frame
        start = jnp.int32(0)
        for length, end in zip(lengths, ends):
            start = start + jnp.where(end <= at, length, 0)
        return at - lag >= start

    def add(lag, value, start, stop):
        for frame in range(start, stop):
            part = value[(frame - start) * BLK:(frame - start + 1) * BLK]
            if lag:
                part = jnp.where(live(frame, lag), part, 0.0)
            conv[frame] += part

    for frame in (4, 5, 3, 2):
        for row in (1, 2):
            spread(frame, row)
    for frame in range(NB):
        conv[frame] = (
            feats_ref[frame].reshape(BLK, channels).astype(jnp.float32) + bias_ref[...].reshape(1, channels))
    weight_copies[0].wait()
    add(0, product(0, 1, 0, NB), 0, NB)
    for lag in (1, 2):
        weight_copies[lag].wait()
        add(lag, product(lag, 1, 2, NB), 2, NB)

    def received(k):
        gets_it, copy = rims[k][1], rims[k][2]

        @pl.when(gets_it)
        def _():
            copy.wait_recv()

    for k in (0, 1):
        received(k)
        send_rim(k + 5)
    for frame in (4, 5):
        for row in (0, 3):
            spread(frame, row)
    add(0, product(0, 0, 2, NB) + product(0, 2, 2, NB), 2, NB)
    for k in (2, 3):
        received(k)
    for frame in (2, 3):
        for row in (0, 3):
            spread(frame, row)
    for lag in (1, 2):
        add(lag, product(lag, 0, 2, NB) + product(lag, 2, 2, NB), 2, NB)

    def dispatch(i):
        return pltpu.make_async_remote_copy(
            src_ref=resid_ref.at[i], dst_ref=rin.at[slot], send_sem=a_send.at[i],
            recv_sem=a_recv.at[slot], device_id=partner(PLACE[i]), device_id_type=MESH)

    def bring_back(l):
        return pltpu.make_async_remote_copy(
            src_ref=stage.at[l], dst_ref=out_hbm.at[home_frame], send_sem=r_send.at[l],
            recv_sem=r_recv.at[home_frame], device_id=partner(origin(l)), device_id_type=MESH)

    def put_back(l):
        return pltpu.make_async_copy(stage.at[l], out_hbm.at[home_frame], o_sem.at[NB])

    def arrival(k, target, recv_sem):
        return pltpu.make_async_remote_copy(
            src_ref=target.at[k], dst_ref=target.at[k], send_sem=a_send.at[k],
            recv_sem=recv_sem.at[k], device_id=sibling, device_id_type=MESH)

    resid_copies = [
        pltpu.make_async_copy(resid_ref.at[i], resid_hbm.at[i], o_sem.at[i]) for i in range(NB)]

    def hand_over(i):
        resid_ref[i] = conv[i].astype(jnp.bfloat16)
        resid_copies[i].start()

        @pl.when(remote(PLACE[i]))
        def _():
            dispatch(i).start()

        @pl.when(jnp.logical_not(remote(PLACE[i])))
        def _():
            rin[PLACE[i]] = resid_ref[i]

    hand_over(2)
    hand_over(3)
    add(0, product(0, 0, 0, 2) + product(0, 2, 0, 2), 0, 2)
    for k in (4, 5, 6):
        received(k)
    for frame in range(2):
        for row in range(4):
            spread(frame, row)
    for lag in (1, 2):
        add(lag, product(lag, 0, 0, 2) + product(lag, 1, 0, 2) + product(lag, 2, 0, 2), 0, 2)
    hand_over(0)
    hand_over(1)

    sends = []

    def block(group, place):
        return kv.at[group, pl.ds(place * BLK, BLK)]

    def push(source, dest, device):
        copy = pltpu.make_async_remote_copy(
            src_ref=block(*source), dst_ref=block(*dest),
            send_sem=g_send.at[len(sends)], recv_sem=g_recv.at[dest[0] * 8 + dest[1]],
            device_id=device, device_id_type=MESH)
        copy.start()
        sends.append(copy)

    def landed(group, place):
        pltpu.make_async_remote_copy(
            src_ref=block(group, place), dst_ref=block(group, place),
            send_sem=g_send.at[0], recv_sem=g_recv.at[group * 8 + place],
            device_id=sibling, device_id_type=MESH).wait_recv()

    home = {0: (1, 0), 2: (1, 1), 1: (2, 0), 3: (2, 1)}

    def normalise(l):
        b = origin(l)

        @pl.when(remote(b))
        def _():
            arrival(b, rin, a_recv).wait_recv()

        kv[0, l * BLK:(l + 1) * BLK] = scaled(rin[b].astype(jnp.float32), attn_gain).astype(jnp.bfloat16)
        group, place = home[l]
        push((0, l), (group, place), right)
        push((0, l), (group, 2 + place), left)
        push((0, l), (0, 4 + l), sibling)

    for l in TURN:
        normalise(l)

    for copy in small_copies:
        copy.wait()
    queries = jnp.dot(kv[0, 0:ROWS], wq_ref[...], preferred_element_type=jnp.float32).astype(jnp.bfloat16)
    folded = lax.dot_general(
        queries, wk_ref[...], (((1,), (1,)), ((), ())), preferred_element_type=jnp.float32)
    qs[...] = (folded * (math.log2(math.e) / math.sqrt(folded.shape[-1]))).astype(jnp.bfloat16)
    top[...] = jnp.full_like(top, -1e30)
    total[...] = jnp.zeros_like(total)
    acc[...] = jnp.zeros_like(acc)

    def attend(group, tile, begin=0, end=2 * ROWS):
        at = slice(tile * TILE, (tile + 1) * TILE)
        keys = kv[group, begin:end]
        scores = lax.dot_general(
            qs[at], keys, (((1,), (1,)), ((), ())), preferred_element_type=jnp.float32)
        pieces = [scores[:, k:k + 128] for k in range(0, end - begin, 128)]
        lanes = pieces[0]
        for piece in pieces[1:]:
            lanes = jnp.maximum(lanes, piece)
        old = top[at]
        new = jnp.maximum(old, jnp.broadcast_to(jnp.max(lanes, axis=-1, keepdims=True), old.shape))
        rescale = jnp.exp2(old - new)
        expanded = [jnp.exp2(piece - new) for piece in pieces]
        parts = expanded[0]
        for piece in expanded[1:]:
            parts = parts + piece
        total[at] = total[at] * rescale + parts
        top[at] = new
        weights = jnp.concatenate([piece.astype(jnp.bfloat16) for piece in expanded], axis=1)
        summed = jnp.dot(weights, keys, preferred_element_type=jnp.float32)
        for k in range(0, channels, 128):
            acc[at, k:k + 128] = acc[at, k:k + 128] * rescale + summed[:, k:k + 128]

    tiles = range(ROWS // TILE)
    for b in range(NB):
        landed(0, 4 + b)
    for tile in tiles:
        attend(0, tile)
    for group, from_left, from_right in ((1, 0, 2), (2, 1, 3)):
        for place, forward, device in ((0, from_left, right), (3, from_right, left), (1, None, None), (2, None, None)):
            landed(group, place)
            if forward is not None:
                push((group, place), (3, forward), device)
            push((group, place), (group, 4 + place), sibling)
        for place in range(4):
            landed(group, 4 + place)
        for tile in tiles:
            attend(group, tile)
    for b in (0, 2, 1, 3):
        landed(3, b)
        push((3, b), (3, 4 + b), sibling)
    attend(3, 0, 0, ROWS)
    for b in range(NB):
        landed(3, 4 + b)

    for tile in tiles:
        if tile:
            attend(3, tile, 0, ROWS)
        attend(3, tile, ROWS, 2 * ROWS)
        at = slice(tile * TILE, (tile + 1) * TILE)
        whole = jnp.sum(total[at], axis=-1, keepdims=True)
        mixture = (acc[at] / whole).astype(jnp.bfloat16)
        attended = jnp.dot(mixture, wv_ref[...], preferred_element_type=jnp.float32).astype(jnp.bfloat16)
        update = jnp.dot(attended, wo_ref[...], preferred_element_type=jnp.float32)
        for half in range(TILE // BLK):
            l = tile * (TILE // BLK) + half
            stage[l] = (
                rin[origin(l)].astype(jnp.float32) + update[half * BLK:(half + 1) * BLK]).astype(jnp.bfloat16)

            @pl.when(remote(origin(l)))
            def _(l=l):
                bring_back(l).start()

            @pl.when(jnp.logical_not(remote(origin(l))))
            def _(l=l):
                put_back(l).start()

    for copy in sends:
        copy.wait_send()
    for sends_it, _, copy, _ in rims:
        @pl.when(sends_it)
        def _(copy=copy):
            copy.wait_send()
    for b in range(NB):
        @pl.when(remote(b))
        def _(b=b):
            dispatch(FRAME[b]).wait_send()
            arrival(FRAME[b], out_hbm, r_recv).wait_recv()

        @pl.when(remote(origin(b)))
        def _(b=b):
            bring_back(b).wait_send()

        @pl.when(jnp.logical_not(remote(origin(b))))
        def _(b=b):
            put_back(b).wait()
        resid_copies[b].wait()


def finish_kernel(resid_ref, mixed_ref, resid_out, mixed_out, held, in_sems, out_sems):
    pairs = [(resid_ref, resid_out), (mixed_ref, mixed_out)]
    fetched = [pltpu.make_async_copy(pairs[k][0], held.at[k], in_sems.at[k]) for k in range(2)]
    stored = [pltpu.make_async_copy(held.at[k], pairs[k][1], out_sems.at[k]) for k in range(2)]
    for copy in fetched:
        copy.start()
    for first, second in zip(fetched, stored):
        first.wait()
        second.start()
    for copy in stored:
        copy.wait()


def local(
    feats, clip_lengths, norm_gain, conv_weight, conv_bias, attn_gain,
    query_weight, key_weight, value_weight, output_weight,
):
    channels = feats.shape[-1]
    vmem = pl.BlockSpec(memory_space=pltpu.VMEM)
    smem = pl.BlockSpec(memory_space=pltpu.SMEM)
    hbm = pl.BlockSpec(memory_space=pl.ANY)
    dma = pltpu.SemaphoreType.DMA
    half = jax.ShapeDtypeStruct((NB, BLK, channels), jnp.bfloat16)
    resid, mixed = pl.pallas_call(
        block_kernel,
        out_shape=(half, half),
        in_specs=[smem] + [vmem] * 3 + [hbm] * 6,
        out_specs=(hbm, hbm),
        scratch_shapes=[
            pltpu.VMEM(feats.shape, jnp.bfloat16),
        ] + [pltpu.VMEM((channels, channels), jnp.bfloat16)] * 4 + [
            pltpu.VMEM((3, 3, 3 * channels, channels), jnp.bfloat16),
            pltpu.VMEM((NB + 2, 4, COLS, channels), jnp.bfloat16),
            pltpu.VMEM((NB + 2, 4, COLS, 3 * channels), jnp.bfloat16),
            pltpu.VMEM((NB, BLK, channels), jnp.float32),
            pltpu.VMEM((NB, BLK, channels), jnp.bfloat16),
            pltpu.VMEM((NB, BLK, channels), jnp.bfloat16),
            pltpu.VMEM((4, 2 * ROWS, channels), jnp.bfloat16),
            pltpu.VMEM((ROWS, channels), jnp.bfloat16),
            pltpu.VMEM((ROWS, channels), jnp.float32),
            pltpu.VMEM((ROWS, 128), jnp.float32),
            pltpu.VMEM((ROWS, 128), jnp.float32),
            pltpu.VMEM((NB, BLK, channels), jnp.bfloat16),
            dma, dma((4,)), dma((3,)), dma((NB + 1,)), dma((7,)), dma((7,)), dma((NB,)), dma((NB,)),
            dma((28,)), dma((32,)), dma((NB,)), dma((NB,)),
        ],
        compiler_params=pltpu.CompilerParams(
            collective_id=1, has_side_effects=True, vmem_limit_bytes=56 * 1024 * 1024),
        cost_estimate=pl.CostEstimate(
            flops=16_000_000_000, bytes_accessed=12_000_000, transcendentals=4_000_000),
    )(
        clip_lengths, norm_gain, conv_bias, attn_gain, feats,
        conv_weight.reshape(3, 3, 3 * channels, channels),
        query_weight, key_weight, value_weight, output_weight,
    )
    resid, mixed = pl.pallas_call(
        finish_kernel,
        out_shape=(half, half),
        in_specs=[hbm, hbm],
        out_specs=(hbm, hbm),
        scratch_shapes=[pltpu.VMEM((2, NB, BLK, channels), jnp.bfloat16), dma((2,)), dma((2,))],
        compiler_params=pltpu.CompilerParams(vmem_limit_bytes=60 * 1024 * 1024),
    )(resid, mixed)
    return resid.reshape(feats.shape), mixed.reshape(feats.shape)


def solution(mesh):
    return jax.shard_map(
        local,
        mesh=mesh,
        in_specs=(P("tm", "space", None, None), P(), P(), P(), P(), P(), P(), P(), P(), P()),
        out_specs=(P("tm", "space", None, None), P("tm", "space", None, None)),
        check_vma=False,
    )
```

```python
import math

import jax
import jax.numpy as jnp
from jax import lax
from jax.experimental import pallas as pl
from jax.experimental.pallas import tpu as pltpu
from jax.sharding import PartitionSpec as P

MESH = pl.DeviceIdType.MESH
COLS = 80
BLK = 2 * COLS
NB = 4
ROWS = NB * BLK
TILE = 320
PLACE = (1, 3, 0, 2)
FRAME = (2, 0, 3, 1)
TURN = (0, 2, 1, 3)


def scaled(wide, gain):
    mean = jnp.mean(wide * wide, axis=-1, keepdims=True)
    return wide * lax.rsqrt(mean + 1e-06) * gain


def block_kernel(
    clip_ref, norm_gain_ref, bias_ref, gain_ref, feats_hbm, conv_hbm, wq_hbm, wk_hbm, wv_hbm, wo_hbm,
    resid_hbm, out_hbm,
    feats_ref, wq_ref, wk_ref, wv_ref, wo_ref,
    weight, active, taps, conv, resid_ref, rin, kv, qs, acc, top, total, stage,
    f_sem, p_sem, w_sem, o_sem, h_send, h_recv, a_send, a_recv, g_send, g_recv, r_send, r_recv,
):
    tm, space = lax.axis_index("tm"), lax.axis_index("space")
    y, c = tm // 2, tm % 2
    z, x = space // 4, space % 4
    right = (tm, 4 * z + (x + 1) % 4)
    left = (tm, 4 * z + (x + 3) % 4)
    sibling = (2 * y + 1 - c, space)
    slot, core = z % 4, z // 4
    above, below = (space + 31) % 32, (space + 1) % 32
    later, earlier = (tm + 1) % 8, (tm + 7) % 8
    channels = feats_ref.shape[-1]

    home_frame = slot // 2 + 2 * (1 - slot % 2)

    def partner(p):
        return (2 * y + core, 4 * (4 * c + p) + x)

    def remote(p):
        return 4 * c + p != z

    away, step = (core + c) % 2, 1 - 2 * (slot // 2)

    def origin(l):
        turn = TURN[l] + away * (3 - 2 * TURN[l])
        return (slot + step * turn + 8) % 4

    feats_copy = pltpu.make_async_copy(feats_hbm, feats_ref, f_sem)
    feats_copy.start()
    weight_copies = [
        pltpu.make_async_copy(conv_hbm.at[lag], weight.at[lag], w_sem.at[lag]) for lag in range(3)]
    small_copies = [
        pltpu.make_async_copy(source, target, p_sem.at[k])
        for k, (source, target) in enumerate(
            ((wq_hbm, wq_ref), (wk_hbm, wk_ref), (wv_hbm, wv_ref), (wo_hbm, wo_ref)))]
    for copy in weight_copies + small_copies:
        copy.start()

    barrier = pltpu.get_barrier_semaphore()
    for device in (
        left, right, sibling, (tm, above), (tm, below), (later, space), (earlier, space),
    ):
        pl.semaphore_signal(barrier, inc=1, device_id=device, device_id_type=MESH)
    for i in range(NB):
        @pl.when(remote(i))
        def _(i=i):
            pl.semaphore_signal(barrier, inc=1, device_id=partner(i), device_id_type=MESH)

    feats_copy.wait()
    norm_gain = norm_gain_ref[...].reshape(1, channels)
    attn_gain = gain_ref[...].reshape(1, channels)

    def activate(frame):
        for row in range(2):
            unit = scaled(feats_ref[frame, row].astype(jnp.float32), norm_gain)
            active[frame + 2, row + 1] = (unit / (1.0 + jnp.exp(-unit))).astype(jnp.bfloat16)

    for frame in (2, 3):
        activate(frame)

    @pl.when(core == c)
    def _():
        pl.semaphore_wait(barrier, 10)

    @pl.when(core != c)
    def _():
        pl.semaphore_wait(barrier, 11)

    older, recent = pl.ds(2, 2), pl.ds(4, 2)
    first = pl.ds(0, 2)
    has_above, has_below, has_earlier, has_later = space > 0, space < 31, tm > 0, tm < 7

    def rim(k, source, target, device):
        return pltpu.make_async_remote_copy(
            src_ref=active.at[source[0], source[1]], dst_ref=active.at[target[0], target[1]],
            send_sem=h_send.at[k], recv_sem=h_recv.at[k], device_id=device, device_id_type=MESH)

    top_row, low_row, both_rows = pl.ds(1, 1), pl.ds(2, 1), pl.ds(1, 2)
    before_row, after_row = pl.ds(0, 1), pl.ds(3, 1)
    rims = [
        (has_below, has_above, rim(0, (recent, low_row), (recent, before_row), (tm, below)), (recent, before_row)),
        (has_above, has_below, rim(1, (recent, top_row), (recent, after_row), (tm, above)), (recent, after_row)),
        (has_below, has_above, rim(2, (older, low_row), (older, before_row), (tm, below)), (older, before_row)),
        (has_above, has_below, rim(3, (older, top_row), (older, after_row), (tm, above)), (older, after_row)),
        (has_later, has_earlier, rim(4, (recent, both_rows), (first, both_rows), (later, space)), (first, both_rows)),
        (jnp.logical_and(has_later, has_above), jnp.logical_and(has_earlier, has_above),
         rim(5, (recent, before_row), (first, before_row), (later, space)), (first, before_row)),
        (jnp.logical_and(has_later, has_below), jnp.logical_and(has_earlier, has_below),
         rim(6, (recent, after_row), (first, after_row), (later, space)), (first, after_row)),
    ]

    def send_rim(k):
        @pl.when(rims[k][0])
        def _():
            rims[k][2].start()

    for k in (0, 1, 4):
        send_rim(k)
    for frame in (0, 1):
        activate(frame)
    for k in (2, 3):
        send_rim(k)
    for sends_it, gets_it, copy, place in rims:
        @pl.when(jnp.logical_not(gets_it))
        def _(place=place):
            hole = active.at[place[0], place[1]]
            hole[...] = jnp.zeros_like(hole)

    column = lax.broadcasted_iota(jnp.int32, (COLS, channels), 0)

    def spread(frame, row):
        middle = active[frame, row]
        wide = middle.astype(jnp.float32)
        taps[frame, row, :, 0:channels] = jnp.where(
            column == 0, 0.0, pltpu.roll(wide, 1, 0)).astype(jnp.bfloat16)
        taps[frame, row, :, channels:2 * channels] = middle
        taps[frame, row, :, 2 * channels:3 * channels] = jnp.where(
            column == COLS - 1, 0.0, pltpu.roll(wide, COLS - 1, 0)).astype(jnp.bfloat16)

    def product(lag, offset, start, stop):
        window = taps[start + 2 - lag:stop + 2 - lag, offset:offset + 2]
        return jnp.dot(
            window.reshape((stop - start) * BLK, 3 * channels), weight[lag, offset],
            preferred_element_type=jnp.float32)

    lengths = [clip_ref[k] for k in range(3)]
    ends = [lengths[0], lengths[0] + lengths[1], lengths[0] + lengths[1] + lengths[2]]

    def live(frame, lag):
        at = tm * NB + frame
        start = jnp.int32(0)
        for length, end in zip(lengths, ends):
            start = start + jnp.where(end <= at, length, 0)
        return at - lag >= start

    def add(lag, value, start, stop):
        for frame in range(start, stop):
            part = value[(frame - start) * BLK:(frame - start + 1) * BLK]
            if lag:
                part = jnp.where(live(frame, lag), part, 0.0)
            conv[frame] += part

    for frame in (4, 5, 3, 2):
        for row in (1, 2):
            spread(frame, row)
    for frame in range(NB):
        conv[frame] = (
            feats_ref[frame].reshape(BLK, channels).astype(jnp.float32) + bias_ref[...].reshape(1, channels))
    weight_copies[0].wait()
    add(0, product(0, 1, 0, NB), 0, NB)
    for lag in (1, 2):
        weight_copies[lag].wait()
        add(lag, product(lag, 1, 2, NB), 2, NB)

    def received(k):
        gets_it, copy = rims[k][1], rims[k][2]

        @pl.when(gets_it)
        def _():
            copy.wait_recv()

    for k in (0, 1):
        received(k)
        send_rim(k + 5)
    for frame in (4, 5):
        for row in (0, 3):
            spread(frame, row)
    add(0, product(0, 0, 2, NB) + product(0, 2, 2, NB), 2, NB)
    for k in (2, 3):
        received(k)
    for frame in (2, 3):
        for row in (0, 3):
            spread(frame, row)
    for lag in (1, 2):
        add(lag, product(lag, 0, 2, NB) + product(lag, 2, 2, NB), 2, NB)

    def dispatch(i):
        return pltpu.make_async_remote_copy(
            src_ref=resid_ref.at[i], dst_ref=rin.at[slot], send_sem=a_send.at[i],
            recv_sem=a_recv.at[slot], device_id=partner(PLACE[i]), device_id_type=MESH)

    def bring_back(l):
        return pltpu.make_async_remote_copy(
            src_ref=stage.at[l], dst_ref=out_hbm.at[home_frame], send_sem=r_send.at[l],
            recv_sem=r_recv.at[home_frame], device_id=partner(origin(l)), device_id_type=MESH)

    def put_back(l):
        return pltpu.make_async_copy(stage.at[l], out_hbm.at[home_frame], o_sem.at[NB])

    def arrival(k, target, recv_sem):
        return pltpu.make_async_remote_copy(
            src_ref=target.at[k], dst_ref=target.at[k], send_sem=a_send.at[k],
            recv_sem=recv_sem.at[k], device_id=sibling, device_id_type=MESH)

    resid_copies = [
        pltpu.make_async_copy(resid_ref.at[i], resid_hbm.at[i], o_sem.at[i]) for i in range(NB)]

    def hand_over(i):
        resid_ref[i] = conv[i].astype(jnp.bfloat16)
        resid_copies[i].start()

        @pl.when(remote(PLACE[i]))
        def _():
            dispatch(i).start()

        @pl.when(jnp.logical_not(remote(PLACE[i])))
        def _():
            rin[PLACE[i]] = resid_ref[i]

    hand_over(2)
    hand_over(3)
    add(0, product(0, 0, 0, 2) + product(0, 2, 0, 2), 0, 2)
    for k in (4, 5, 6):
        received(k)
    for frame in range(2):
        for row in range(4):
            spread(frame, row)
    for lag in (1, 2):
        add(lag, product(lag, 0, 0, 2) + product(lag, 1, 0, 2) + product(lag, 2, 0, 2), 0, 2)
    hand_over(0)
    hand_over(1)

    sends = []

    def block(group, place):
        return kv.at[group, pl.ds(place * BLK, BLK)]

    def push(source, dest, device):
        copy = pltpu.make_async_remote_copy(
            src_ref=block(*source), dst_ref=block(*dest),
            send_sem=g_send.at[len(sends)], recv_sem=g_recv.at[dest[0] * 8 + dest[1]],
            device_id=device, device_id_type=MESH)
        copy.start()
        sends.append(copy)

    def landed(group, place):
        pltpu.make_async_remote_copy(
            src_ref=block(group, place), dst_ref=block(group, place),
            send_sem=g_send.at[0], recv_sem=g_recv.at[group * 8 + place],
            device_id=sibling, device_id_type=MESH).wait_recv()

    home = {0: (1, 0), 2: (1, 1), 1: (2, 0), 3: (2, 1)}

    def normalise(l):
        b = origin(l)

        @pl.when(remote(b))
        def _():
            arrival(b, rin, a_recv).wait_recv()

        kv[0, l * BLK:(l + 1) * BLK] = scaled(rin[b].astype(jnp.float32), attn_gain).astype(jnp.bfloat16)
        group, place = home[l]
        push((0, l), (group, place), right)
        push((0, l), (group, 2 + place), left)
        push((0, l), (0, 4 + l), sibling)

    for l in TURN:
        normalise(l)

    for copy in small_copies:
        copy.wait()
    queries = jnp.dot(kv[0, 0:ROWS], wq_ref[...], preferred_element_type=jnp.float32).astype(jnp.bfloat16)
    folded = lax.dot_general(
        queries, wk_ref[...], (((1,), (1,)), ((), ())), preferred_element_type=jnp.float32)
    qs[...] = (folded * (math.log2(math.e) / math.sqrt(folded.shape[-1]))).astype(jnp.bfloat16)
    top[...] = jnp.full_like(top, -1e30)
    total[...] = jnp.zeros_like(total)
    acc[...] = jnp.zeros_like(acc)

    def attend(group, tile, begin=0, end=2 * ROWS):
        at = slice(tile * TILE, (tile + 1) * TILE)
        keys = kv[group, begin:end]
        scores = lax.dot_general(
            qs[at], keys, (((1,), (1,)), ((), ())), preferred_element_type=jnp.float32)
        pieces = [scores[:, k:k + 128] for k in range(0, end - begin, 128)]
        lanes = pieces[0]
        for piece in pieces[1:]:
            lanes = jnp.maximum(lanes, piece)
        old = top[at]
        new = jnp.maximum(old, jnp.broadcast_to(jnp.max(lanes, axis=-1, keepdims=True), old.shape))
        rescale = jnp.exp2(old - new)
        expanded = [jnp.exp2(piece - new) for piece in pieces]
        parts = expanded[0]
        for piece in expanded[1:]:
            parts = parts + piece
        total[at] = total[at] * rescale + parts
        top[at] = new
        weights = jnp.concatenate([piece.astype(jnp.bfloat16) for piece in expanded], axis=1)
        summed = jnp.dot(weights, keys, preferred_element_type=jnp.float32)
        for k in range(0, channels, 128):
            acc[at, k:k + 128] = acc[at, k:k + 128] * rescale + summed[:, k:k + 128]

    tiles = range(ROWS // TILE)
    for b in range(NB):
        landed(0, 4 + b)
    for tile in tiles:
        attend(0, tile)
    def relay(group, from_left, from_right):
        for place, forward, device in ((0, from_left, right), (3, from_right, left), (1, None, None), (2, None, None)):
            landed(group, place)
            if forward is not None:
                push((group, place), (3, forward), device)
            push((group, place), (group, 4 + place), sibling)

    relay(1, 0, 2)
    for place in range(4):
        landed(1, 4 + place)
    attend(1, 0)
    relay(2, 1, 3)
    for tile in tiles[1:]:
        attend(1, tile)
    for place in range(4):
        landed(2, 4 + place)
    for tile in tiles:
        attend(2, tile)
    for b in (0, 2, 1, 3):
        landed(3, b)
        push((3, b), (3, 4 + b), sibling)
    attend(3, 0, 0, ROWS)
    for b in range(NB):
        landed(3, 4 + b)

    for tile in tiles:
        if tile:
            attend(3, tile, 0, ROWS)
        attend(3, tile, ROWS, 2 * ROWS)
        at = slice(tile * TILE, (tile + 1) * TILE)
        whole = jnp.sum(total[at], axis=-1, keepdims=True)
        mixture = (acc[at] / whole).astype(jnp.bfloat16)
        attended = jnp.dot(mixture, wv_ref[...], preferred_element_type=jnp.float32).astype(jnp.bfloat16)
        update = jnp.dot(attended, wo_ref[...], preferred_element_type=jnp.float32)
        for half in range(TILE // BLK):
            l = tile * (TILE // BLK) + half
            stage[l] = (
                rin[origin(l)].astype(jnp.float32) + update[half * BLK:(half + 1) * BLK]).astype(jnp.bfloat16)

            @pl.when(remote(origin(l)))
            def _(l=l):
                bring_back(l).start()

            @pl.when(jnp.logical_not(remote(origin(l))))
            def _(l=l):
                put_back(l).start()

    for copy in sends:
        copy.wait_send()
    for sends_it, _, copy, _ in rims:
        @pl.when(sends_it)
        def _(copy=copy):
            copy.wait_send()
    for b in range(NB):
        @pl.when(remote(b))
        def _(b=b):
            dispatch(FRAME[b]).wait_send()
            arrival(FRAME[b], out_hbm, r_recv).wait_recv()

        @pl.when(remote(origin(b)))
        def _(b=b):
            bring_back(b).wait_send()

        @pl.when(jnp.logical_not(remote(origin(b))))
        def _(b=b):
            put_back(b).wait()
        resid_copies[b].wait()


def finish_kernel(resid_ref, mixed_ref, resid_out, mixed_out, held, in_sems, out_sems):
    pairs = [(resid_ref, resid_out), (mixed_ref, mixed_out)]
    fetched = [pltpu.make_async_copy(pairs[k][0], held.at[k], in_sems.at[k]) for k in range(2)]
    stored = [pltpu.make_async_copy(held.at[k], pairs[k][1], out_sems.at[k]) for k in range(2)]
    for copy in fetched:
        copy.start()
    for first, second in zip(fetched, stored):
        first.wait()
        second.start()
    for copy in stored:
        copy.wait()


def local(
    feats, clip_lengths, norm_gain, conv_weight, conv_bias, attn_gain,
    query_weight, key_weight, value_weight, output_weight,
):
    channels = feats.shape[-1]
    vmem = pl.BlockSpec(memory_space=pltpu.VMEM)
    smem = pl.BlockSpec(memory_space=pltpu.SMEM)
    hbm = pl.BlockSpec(memory_space=pl.ANY)
    dma = pltpu.SemaphoreType.DMA
    half = jax.ShapeDtypeStruct((NB, BLK, channels), jnp.bfloat16)
    resid, mixed = pl.pallas_call(
        block_kernel,
        out_shape=(half, half),
        in_specs=[smem] + [vmem] * 3 + [hbm] * 6,
        out_specs=(hbm, hbm),
        scratch_shapes=[
            pltpu.VMEM(feats.shape, jnp.bfloat16),
        ] + [pltpu.VMEM((channels, channels), jnp.bfloat16)] * 4 + [
            pltpu.VMEM((3, 3, 3 * channels, channels), jnp.bfloat16),
            pltpu.VMEM((NB + 2, 4, COLS, channels), jnp.bfloat16),
            pltpu.VMEM((NB + 2, 4, COLS, 3 * channels), jnp.bfloat16),
            pltpu.VMEM((NB, BLK, channels), jnp.float32),
            pltpu.VMEM((NB, BLK, channels), jnp.bfloat16),
            pltpu.VMEM((NB, BLK, channels), jnp.bfloat16),
            pltpu.VMEM((4, 2 * ROWS, channels), jnp.bfloat16),
            pltpu.VMEM((ROWS, channels), jnp.bfloat16),
            pltpu.VMEM((ROWS, channels), jnp.float32),
            pltpu.VMEM((ROWS, 128), jnp.float32),
            pltpu.VMEM((ROWS, 128), jnp.float32),
            pltpu.VMEM((NB, BLK, channels), jnp.bfloat16),
            dma, dma((4,)), dma((3,)), dma((NB + 1,)), dma((7,)), dma((7,)), dma((NB,)), dma((NB,)),
            dma((28,)), dma((32,)), dma((NB,)), dma((NB,)),
        ],
        compiler_params=pltpu.CompilerParams(
            collective_id=1, has_side_effects=True, vmem_limit_bytes=56 * 1024 * 1024),
        cost_estimate=pl.CostEstimate(
            flops=16_000_000_000, bytes_accessed=12_000_000, transcendentals=4_000_000),
    )(
        clip_lengths, norm_gain, conv_bias, attn_gain, feats,
        conv_weight.reshape(3, 3, 3 * channels, channels),
        query_weight, key_weight, value_weight, output_weight,
    )
    resid, mixed = pl.pallas_call(
        finish_kernel,
        out_shape=(half, half),
        in_specs=[hbm, hbm],
        out_specs=(hbm, hbm),
        scratch_shapes=[pltpu.VMEM((2, NB, BLK, channels), jnp.bfloat16), dma((2,)), dma((2,))],
        compiler_params=pltpu.CompilerParams(vmem_limit_bytes=60 * 1024 * 1024),
    )(resid, mixed)
    return resid.reshape(feats.shape), mixed.reshape(feats.shape)


def solution(mesh):
    return jax.shard_map(
        local,
        mesh=mesh,
        in_specs=(P("tm", "space", None, None), P(), P(), P(), P(), P(), P(), P(), P(), P()),
        out_specs=(P("tm", "space", None, None), P("tm", "space", None, None)),
        check_vma=False,
    )
```
